256 devices in a mesh: row: 128 (over y, z, x), col: 2 (over core).
Axes of the slice: x: 4, y: 4, z: 8, core: 2. Of those that a mesh axis runs over, the one named last changes fastest.
Arguments:
- tiles: bfloat16 [128, 2, 256, 128, 128], P('row', 'col'), may hold values from -0.0625 to 0.0625
- tile_rows: int32 [128, 2, 256], P('row', 'col'), may hold values from 0 to 3
- tile_cols: int32 [128, 2, 256], P('row', 'col'), may hold values from 0 to 255
- tile_counts: int32 [128, 2], P('row', 'col'), may hold values from 1 to 256, as said below
- degrees: float32 [65536], P(('row', 'col')), may hold values from 0.5 to 2
- start_block: float32 [64, 65536], P(None, ('row', 'col')), may hold values from -6 to 6
Outputs:
- basis: float32 [64, 65536], P(None, ('row', 'col'))
- coefficients: float32 [3, 64, 128], replicated
The draws below stay inside these ranges and needn't reach their ends.
Inputs may be any that keep to these rules, and one draw needn't show every extreme that they name: `tile_counts`: some device has all 256 slots live.
All inputs are finite; a program needn't handle non-finite values.
Results may differ from the reference program's by a relative error of at most 0.0045.
Values may be sent and summed in bfloat16 or wider, within the bound.
No kernel may reach another device: no remote copies, remote signals or barrier semaphores. Data moves between devices by JAX's collectives and lax.ppermute only.
A program may use at most 64 MiB of HBM per device.

```python
import math
import jax
import jax.numpy as jnp
from jax import lax

K = 64
RB = 4
SLOTS = 256
ITERS = 3
NODES = 65536
COLB = 256
N_ROW = 128
N_COL = 2


def draw_tile_counts(key, part):
    key = jax.random.fold_in(key, 7)
    first_key, second_key, third_key = jax.random.split(key, 3)
    grid_shape = (N_ROW, N_COL)
    first_draw = jax.random.randint(first_key, grid_shape, 1, SLOTS + 1)
    second_draw = jax.random.randint(second_key, grid_shape, 1, SLOTS + 1)
    counts = jnp.minimum(first_draw, second_draw).reshape(-1)
    full_index = jax.random.randint(third_key, (), 0, N_ROW * N_COL)
    counts = jnp.where(jnp.arange(N_ROW * N_COL) == full_index, SLOTS, counts)
    return counts.reshape(grid_shape).astype(jnp.int32)


def touch_ends(values, own_key, smallest, largest):
    spot = [jax.random.randint(jax.random.fold_in(own_key, axis), (), 0, length) for axis, length in enumerate(values.shape)]
    widest = values.shape.index(max(values.shape))
    beside = spot[:widest] + [(spot[widest] + 1) % values.shape[widest]] + spot[widest + 1:]
    return values.at[tuple(spot)].set(smallest).at[tuple(beside)].set(largest)


def levels(own_key, shape, cuts, low, high):
    factor_of = 1.0
    for position, shards_of in cuts:
        steps = jax.random.uniform(jax.random.fold_in(jax.random.fold_in(own_key, 6), position), (shards_of,), jnp.float32, low / len(cuts), high / len(cuts))
        factor_of = factor_of * jnp.repeat(jnp.exp(steps), shape[position] // shards_of).reshape((-1,) + (1,) * (len(shape) - 1 - position))
    return factor_of


def gaussian(stream_key, shape, width, most, cuts=(), held_as=jnp.bfloat16):
    loudness = levels(stream_key, shape, cuts, -0.22, 0.18) if cuts else 1.0
    array = jax.random.normal(stream_key, shape, jnp.float32) * width * loudness
    return jnp.minimum(jnp.maximum(array, -most), most).astype(held_as)


def setup_inputs(seed: int = 0) -> dict:
    keys = jax.random.split(jax.random.key(seed), 7)
    return {
        "tiles": gaussian(keys[0], (N_ROW, N_COL, SLOTS, 128, 128), (128 * SLOTS // RB) ** -0.5, 0.0625, ((0, 128), (1, 2))),
        "tile_rows": touch_ends(jax.random.randint(keys[1], (N_ROW, N_COL, SLOTS), 0, RB), jax.random.fold_in(keys[1], 1), 0, RB - 1).astype(jnp.int32),
        "tile_cols": touch_ends(jax.random.randint(keys[2], (N_ROW, N_COL, SLOTS), 0, COLB), jax.random.fold_in(keys[2], 1), 0, COLB - 1).astype(jnp.int32),
        "tile_counts": draw_tile_counts(jax.random.fold_in(keys[6], 71), 0),
        "degrees": jnp.clip(jnp.exp(math.log(2.0) - 1.3862944 * jax.random.uniform(keys[4], (NODES,), jnp.float32) ** levels(keys[4], (NODES,), ((0, 256),), -0.2, 0.2)), 0.5, 2.0),
        "start_block": gaussian(keys[5], (K, NODES), 1.0, 6.0, ((1, 256),), jnp.float32),
    }


HIGH = lax.Precision.HIGHEST

def orthonormal(block):
    gram_matrix = jnp.dot(block, block.T, precision=HIGH) / NODES
    factor_low = jnp.linalg.cholesky(gram_matrix)
    new_basis = jax.scipy.linalg.solve_triangular(factor_low, block, lower=True)
    return (new_basis, factor_low)

def device_terms(entry, blocks):
    tile_set, row_ids, col_ids, live_count, core_id = entry
    slot_ids = jnp.arange(SLOTS, dtype=jnp.int32)
    half_rows = RB // 2
    global_cols = col_ids // half_rows * RB + core_id * half_rows + col_ids % half_rows
    columns = jnp.take(blocks, global_cols.astype(jnp.int32), axis=1).astype(jnp.float32)
    contrib = jnp.einsum('ktj,tij->tki', columns, tile_set.astype(jnp.float32), precision=HIGH)
    onehot = ((row_ids[:, None] == jnp.arange(RB, dtype=jnp.int32)[None, :]) & (slot_ids < live_count)[:, None]).astype(jnp.float32)
    return jnp.einsum('tr,tki->kri', onehot, contrib, precision=HIGH)

def adjacency_product(basis, tiles, tile_rows, tile_cols, tile_counts):
    blocks = basis.astype(jnp.bfloat16).reshape(K, NODES // 128, 128)
    devices = N_ROW * N_COL
    packed = (tiles.reshape(devices, SLOTS, 128, 128), tile_rows.reshape(devices, SLOTS), tile_cols.reshape(devices, SLOTS), tile_counts.reshape(devices), (jnp.arange(devices, dtype=jnp.int32) % N_COL).astype(jnp.int32))
    slab_terms = lax.map(lambda entry: device_terms(entry, blocks), packed)
    slab_terms = slab_terms.reshape(N_ROW, N_COL, K, RB, 128).sum(axis=1)
    return jnp.transpose(slab_terms, (1, 0, 2, 3)).reshape(K, NODES)

def reference(tiles, tile_rows, tile_cols, tile_counts, degrees, start_block):
    basis, factor_low = orthonormal(start_block)
    previous = jnp.zeros_like(basis)
    coupling = jnp.zeros((K, K), basis.dtype)
    records = []
    for sweep in range(ITERS):
        product = adjacency_product(basis, tiles, tile_rows, tile_cols, tile_counts)
        image_block = degrees[None, :] * basis - product
        diag_block = jnp.dot(image_block, basis.T, precision=HIGH) / NODES
        residual = image_block - jnp.dot(diag_block, basis, precision=HIGH) - jnp.dot(coupling, previous, precision=HIGH)
        new_basis, factor_low = orthonormal(residual)
        records.append(jnp.concatenate([diag_block, factor_low], axis=1))
        previous, basis, coupling = (basis, new_basis, factor_low.T)
    return (basis, jnp.stack(records))
```

```python
import jax
import jax.numpy as jnp
from jax import lax
from jax.experimental import pallas as pl
from jax.experimental.pallas import tpu as pltpu
from jax.sharding import Mesh, PartitionSpec as P

ITERS = 3
HIGH = lax.Precision.HIGHEST

K = 64
SLOTS = 256
NODES = 65536
SIZES = {"y": 4, "z": 8, "x": 4, "core": 2}
AXES = ("y", "z", "x", "core")
SHIFT = 1.25
AMPLIFY_MAX = 4.0
GRAM = 3

VMEM = pl.BlockSpec(memory_space=pltpu.VMEM)
SMEM = pl.BlockSpec(memory_space=pltpu.SMEM)
ANY = pl.BlockSpec(memory_space=pl.ANY)


def dot(left, right):
    return lax.dot_general(
        left, right, (((1,), (0,)), ((), ())), precision=HIGH, preferred_element_type=jnp.float32
    )


def dot_t(left, right):
    return lax.dot_general(
        left, right, (((1,), (1,)), ((), ())), precision=HIGH, preferred_element_type=jnp.float32
    )


def struct(shape, dtype):
    return jax.ShapeDtypeStruct(shape, dtype)


def put_gram(out_ref, gram):
    high = gram.astype(jnp.bfloat16)
    rest = gram - high.astype(jnp.float32)
    middle = rest.astype(jnp.bfloat16)
    low = (rest - middle.astype(jnp.float32)).astype(jnp.bfloat16)
    out_ref[0] = high
    out_ref[1] = middle
    out_ref[2] = low


def get_gram(ref):
    return (ref[0].astype(jnp.float32) + ref[1].astype(jnp.float32)) + ref[2].astype(jnp.float32)


def put_block(out_ref, block):
    for half in range(2):
        out_ref[GRAM + half] = block[:, half * 128 : (half + 1) * 128].astype(jnp.bfloat16)


def first_kernel(start_ref, out_ref):
    block = start_ref[...]
    gram = dot_t(block, block) * (1.0 / NODES)
    put_gram(out_ref, jnp.concatenate([gram, jnp.zeros_like(gram)], axis=1))
    put_block(out_ref, block)


def merge_kernel(a_ref, b_ref, c_ref, d_ref, out_ref):
    refs = (a_ref, b_ref, c_ref, d_ref)
    count = a_ref.shape[0] - GRAM
    put_gram(
        out_ref, (get_gram(a_ref) + get_gram(b_ref)) + (get_gram(c_ref) + get_gram(d_ref))
    )
    for place, ref in enumerate(refs):
        out_ref[GRAM + place * count : GRAM + (place + 1) * count] = ref[GRAM:]


def merge(parts):
    count = parts[0].shape[0] - GRAM
    return pl.pallas_call(
        merge_kernel,
        out_shape=struct((GRAM + 4 * count, K, 128), jnp.bfloat16),
        in_specs=[VMEM] * 4,
        out_specs=VMEM,
    )(*parts)


def swap(value, axis, mask):
    size = SIZES[axis]
    return lax.ppermute(value, axis, [(i, i ^ mask) for i in range(size)])


def shift(value, axis, step):
    size = SIZES[axis]
    return lax.ppermute(value, axis, [(i, (i + step) % size) for i in range(size)])


def gather(packed):
    for axis in ("x", "y"):
        packed = merge([packed] + [swap(packed, axis, mask) for mask in (1, 2, 3)])
    ups, downs = [packed], [packed]
    for _ in range(3):
        ups.append(shift(ups[-1], "z", 1))
        downs.append(shift(downs[-1], "z", -1))
    cut = 18
    middle = [shift(ups[-1][:cut], "z", 1), shift(downs[-1][cut:], "z", -1)]
    return ups + middle + downs[:0:-1]


def total_kernel(place_ref, *refs):
    pieces, out_ref, held = refs[:8], refs[8], refs[9]
    own = place_ref[0]
    for distance, piece in enumerate(pieces):
        held[lax.rem(own - distance + 8, 8)] = get_gram(piece)
    out_ref[...] = ((held[0] + held[1]) + (held[2] + held[3])) + (
        (held[4] + held[5]) + (held[6] + held[7])
    )


def gram_total(place, pieces):
    heads = pieces[:5] + pieces[6:]
    return pl.pallas_call(
        total_kernel,
        out_shape=struct((K, 128), jnp.float32),
        grid=(1,),
        in_specs=[SMEM]
        + [pl.BlockSpec((GRAM, K, 128), lambda i: (0, 0, 0)) for _ in heads],
        out_specs=pl.BlockSpec((K, 128), lambda i: (0, 0)),
        scratch_shapes=[pltpu.VMEM((8, K, 128), jnp.float32)],
    )(place, *heads)


CHUNK = 32
UNROLL = 8


def tiles_kernel(place_ref, rows_ref, blocks_ref, tiles_ref, *refs):
    pieces, (own_ref, other_ref, held, tiles, sums, piece_sem, tile_sem) = refs[:9], refs[9:]
    copies = []
    offset = 0
    for number, piece in enumerate(pieces):
        skip = 0 if number == 5 else GRAM
        size = piece.shape[0] - skip
        copies.append(
            pltpu.make_async_copy(
                piece.at[pl.ds(skip, size)], held.at[pl.ds(offset, size)], piece_sem.at[number]
            )
        )
        offset += size
    for copy in copies:
        copy.start()
    chunks = [
        pltpu.make_async_copy(
            tiles_ref.at[pl.ds(i * CHUNK, CHUNK)], tiles.at[pl.ds(i * CHUNK, CHUNK)], tile_sem.at[i]
        )
        for i in range(SLOTS // CHUNK)
    ]
    for copy in chunks:
        copy.start()
    sums[...] = jnp.zeros_like(sums)
    live = place_ref[1]
    core = place_ref[2]
    for copy in copies:
        copy.wait()
    for i, copy in enumerate(chunks):
        copy.wait()

        def group(step, carry):
            base = i * CHUNK + step * UNROLL
            products = []
            for u in range(UNROLL):
                products.append(
                    lax.dot_general(
                        held[blocks_ref[base + u]],
                        tiles[base + u],
                        (((1,), (1,)), ((), ())),
                        preferred_element_type=jnp.float32,
                    )
                )
            for u in range(UNROLL):
                row = rows_ref[base + u]
                sums[row] = sums[row] + products[u]
            return carry

        steps = lax.div(jnp.clip(live - i * CHUNK, 0, CHUNK) + UNROLL - 1, UNROLL)
        lax.fori_loop(0, steps, group, 0)
    for half in range(2):
        cols = slice(half * 128, (half + 1) * 128)
        own_ref[:, cols] = sums[2 * core + half]
        other_ref[:, cols] = sums[2 * (1 - core) + half]


def tiles_product(place, rows, blocks, tiles, pieces):
    return pl.pallas_call(
        tiles_kernel,
        out_shape=[struct((K, 256), jnp.float32)] * 2,
        in_specs=[SMEM] * 3 + [ANY] * (1 + len(pieces)),
        out_specs=[VMEM] * 2,
        scratch_shapes=[
            pltpu.VMEM((SLOTS, K, 128), jnp.bfloat16),
            pltpu.VMEM((SLOTS, 128, 128), jnp.bfloat16),
            pltpu.VMEM((5, K, 128), jnp.float32),
            pltpu.SemaphoreType.DMA((len(pieces),)),
            pltpu.SemaphoreType.DMA((SLOTS // CHUNK,)),
        ],
        compiler_params=pltpu.CompilerParams(vmem_limit_bytes=32 * 1024 * 1024),
    )(place, rows, blocks, tiles, *pieces)


def factor_kernel(a_ref, b_ref, spread_ref, row_ref, inverse_ref, spread_out_ref):
    both = a_ref[...] + b_ref[...]
    square, cross = both[:, :K], both[:, K:]
    gram = square - dot_t(cross, cross)
    eye = (
        lax.broadcasted_iota(jnp.int32, (K, K), 0) == lax.broadcasted_iota(jnp.int32, (K, K), 1)
    ).astype(jnp.float32)
    work = jnp.concatenate([gram, eye], axis=1)
    lower = lax.broadcasted_iota(jnp.int32, (K, 128), 0)
    done = []
    for j in range(K):
        pivot = lax.rsqrt(jnp.broadcast_to(work[j : j + 1, j : j + 1], (1, 128)))
        row = work[j : j + 1, :] * pivot
        done.append(row)
        column = work[:, j : j + 1] * pivot[:, :1]
        work = jnp.where(lower > j, work - column * row, work)
    result = jnp.concatenate(done, axis=0)
    below = lax.broadcasted_iota(jnp.int32, (K, K), 0)
    right = lax.broadcasted_iota(jnp.int32, (K, K), 1)
    upper = jnp.where(right >= below, result[:, :K], 0.0)
    inverse = jnp.where(right <= below, result[:, K:], 0.0)
    factor = upper.T
    row_ref[...] = jnp.concatenate([cross + SHIFT * eye, factor], axis=1)
    inverse_ref[...] = jnp.concatenate([inverse, dot(inverse, cross)], axis=1)
    carried = dot(inverse, cross)
    diagonal = jnp.sum(square * eye, axis=1, keepdims=True)
    spread_out_ref[...] = dot(inverse * inverse, jnp.broadcast_to(diagonal, (K, 128))) + dot(
        carried * carried, spread_ref[...]
    )


def factorize(own, other, spread):
    return pl.pallas_call(
        factor_kernel,
        out_shape=[struct((K, 128), jnp.float32)] * 3,
        in_specs=[VMEM] * 3,
        out_specs=[VMEM] * 3,
    )(own, other, spread)


def step_kernel(
    inverse_ref, row_ref, degrees_ref, block_ref, basis_ref, product_ref, own_ref, other_ref,
    new_block_ref, new_basis_ref, new_product_ref, packed_ref,
):
    inverse, carried = inverse_ref[:, :K], inverse_ref[:, K:]
    factor = row_ref[:, K:]
    basis = basis_ref[...]
    new_basis = dot(inverse, block_ref[...]) - dot(carried, basis)
    new_product = dot(inverse, own_ref[...] + other_ref[...]) - dot(carried, product_ref[...])
    block = (degrees_ref[...] - SHIFT) * new_basis - new_product
    block = block - lax.dot_general(
        factor, basis, (((0,), (0,)), ((), ())), precision=HIGH, preferred_element_type=jnp.float32
    )
    new_block_ref[...] = block
    new_basis_ref[...] = new_basis
    new_product_ref[...] = new_product
    gram = dot_t(block, jnp.concatenate([block, new_basis], axis=0)) * (1.0 / NODES)
    put_gram(packed_ref, gram)
    put_block(packed_ref, block)


def step(inverse, row, degrees, block, basis, product, own, other):
    wide = struct((K, 256), jnp.float32)
    return pl.pallas_call(
        step_kernel,
        out_shape=[wide, wide, wide, struct((GRAM + 2, K, 128), jnp.bfloat16)],
        in_specs=[VMEM] * 8,
        out_specs=[VMEM] * 4,
    )(inverse, row, degrees, block, basis, product, own, other)


def last_kernel(inverse_ref, block_ref, basis_ref, out_ref):
    out_ref[...] = dot(inverse_ref[:, :K], block_ref[...]) - dot(inverse_ref[:, K:], basis_ref[...])


def unpack_kernel(packed_ref, out_ref):
    out_ref[...] = get_gram(packed_ref)


def total_over_devices(value):
    for axis, masks in (("x", (1, 2, 3)), ("y", (1, 2, 3)), ("z", (2, 4, 6)), ("z", (1,))):
        parts = [value] + [swap(value, axis, mask) for mask in masks]
        value = parts[0] + parts[1]
        if len(parts) == 4:
            value = value + (parts[2] + parts[3])
    return value


def short_path(tiles, tile_rows, tile_cols, tile_counts, degrees, start_block):
    y, z, x, core = (lax.axis_index(axis) for axis in AXES)
    live = tile_counts.reshape(())
    tile_set = tiles.reshape(SLOTS, 128, 128)
    owner = tile_cols.reshape(-1) // 2
    away = lax.rem(z - owner // 4 % 8 + 8, 8)
    blocks = ((away * 4 + ((owner // 32) ^ y)) * 4 + ((owner % 4) ^ x)) * 2 + tile_cols.reshape(-1) % 2
    rows = jnp.where(jnp.arange(SLOTS, dtype=jnp.int32) < live, tile_rows.reshape(-1), 4)
    place = jnp.stack([z, live, core]).astype(jnp.int32)
    degrees = degrees.reshape(1, -1)

    packed = pl.pallas_call(
        first_kernel,
        out_shape=struct((GRAM + 2, K, 128), jnp.bfloat16),
        in_specs=[VMEM],
        out_specs=VMEM,
    )(start_block)
    block = start_block
    basis = jnp.zeros_like(start_block)
    product = jnp.zeros_like(start_block)
    spread = jnp.zeros((K, 128), jnp.float32)
    records, spreads = [], []
    for sweep in range(ITERS):
        pieces = gather(packed)
        gram = gram_total(place, pieces)
        other_gram = swap(gram, "core", 1)
        own, other = tiles_product(place, rows, blocks, tile_set, pieces)
        other = swap(other, "core", 1)
        row, inverse, spread = factorize(gram, other_gram, spread)
        block, basis, product, packed = step(
            inverse, row, degrees, block, basis, product, own, other
        )
        records.append(row)
        spreads.append(spread)
    gram = pl.pallas_call(
        unpack_kernel,
        out_shape=struct((K, 128), jnp.float32),
        in_specs=[VMEM],
        out_specs=VMEM,
    )(packed)
    gram = total_over_devices(gram)
    row, inverse, spread = factorize(gram, swap(gram, "core", 1), spread)
    records.append(row)
    spreads.append(spread)
    basis = pl.pallas_call(
        last_kernel,
        out_shape=struct((K, 256), jnp.float32),
        in_specs=[VMEM] * 3,
        out_specs=VMEM,
    )(inverse, block, basis)
    return basis, jnp.stack(records[1:]), jnp.max(jnp.stack(spreads))


def tile_terms(totals, blocks, tile_set, row_ids, col_ids, live_count, step_size):
    slab_rows = totals.shape[1]

    def one_block(block_id, running):
        offset = block_id * step_size
        part_tiles = lax.dynamic_slice_in_dim(tile_set, offset, step_size, 0)
        part_rows = lax.dynamic_slice_in_dim(row_ids, offset, step_size, 0)
        part_cols = lax.dynamic_slice_in_dim(col_ids, offset, step_size, 0)
        slot_ids = offset + jnp.arange(step_size, dtype=jnp.int32)
        columns = jnp.take(blocks, part_cols, axis=1)
        contrib = jnp.einsum(
            "ktj,tij->tki", columns, part_tiles, preferred_element_type=jnp.float32
        )
        onehot = (
            (part_rows[:, None] == jnp.arange(slab_rows, dtype=jnp.int32)[None, :])
            & (slot_ids < live_count)[:, None]
        ).astype(jnp.float32)
        return running + jnp.einsum("tr,tki->kri", onehot, contrib, precision=HIGH)

    return lax.fori_loop(0, tile_set.shape[0] // step_size, one_block, totals)


def plain_factorize(block, gram_matrix):
    factor_low = jnp.linalg.cholesky(gram_matrix)
    new_basis = jax.scipy.linalg.solve_triangular(factor_low, block, lower=True)
    return (new_basis, factor_low)


def plain_path(tiles, tile_rows, tile_cols, tile_counts, degrees, start_block):
    vectors = start_block.shape[0]
    own_cols = start_block.shape[1]
    slab_rows = 2 * (own_cols // 128)
    tile_set = tiles.reshape(tiles.shape[2], 128, 128)
    row_ids = tile_rows.reshape(-1)
    col_ids = tile_cols.reshape(-1)
    live_count = tile_counts.reshape(())

    def gram_of(left, right):
        return lax.psum(jnp.dot(left, right.T, precision=HIGH), AXES) / NODES

    basis, factor_low = plain_factorize(start_block, gram_of(start_block, start_block))
    previous = jnp.zeros_like(basis)
    coupling = jnp.zeros((vectors, vectors), jnp.float32)
    records = []
    for sweep in range(ITERS):
        blocks = lax.all_gather(
            basis.astype(jnp.bfloat16), ("y", "z", "x"), axis=1, tiled=True
        ).reshape(vectors, -1, 128)
        totals = jnp.zeros((vectors, slab_rows, 128), jnp.float32)
        totals = tile_terms(totals, blocks, tile_set, row_ids, col_ids, live_count, 32)
        product = lax.psum_scatter(
            totals.reshape(vectors, slab_rows * 128), "core", scatter_dimension=1, tiled=True
        )
        image_block = degrees[None, :] * basis - product
        diag_block = gram_of(image_block, basis)
        residual = (
            image_block
            - jnp.dot(diag_block, basis, precision=HIGH)
            - jnp.dot(coupling, previous, precision=HIGH)
        )
        new_basis, factor_low = plain_factorize(residual, gram_of(residual, residual))
        records.append(jnp.concatenate([diag_block, factor_low], axis=1))
        previous, basis, coupling = (basis, new_basis, factor_low.T)
    return (basis, jnp.stack(records))


def body(*args):
    basis, records, spread = short_path(*args)
    return lax.cond(
        spread < AMPLIFY_MAX, lambda *rest: (basis, records), lambda *rest: plain_path(*rest), *args
    )


def solution(mesh):
    split = Mesh(mesh.devices.reshape(tuple(SIZES[axis] for axis in AXES)), AXES)
    row = ("y", "z", "x")
    in_specs = (
        P(row, "core", None, None, None),
        P(row, "core", None),
        P(row, "core", None),
        P(row, "core"),
        P(AXES),
        P(None, AXES),
    )
    out_specs = (P(None, AXES), P())
    return jax.shard_map(body, mesh=split, in_specs=in_specs, out_specs=out_specs, check_vma=False)
```

```python
import functools

import jax
import jax.numpy as jnp
from jax import lax
from jax.experimental import pallas as pl
from jax.experimental.pallas import tpu as pltpu
from jax.sharding import Mesh, PartitionSpec as P

ITERS = 3
HIGH = lax.Precision.HIGHEST

K = 64
SLOTS = 256
NODES = 65536
SIZES = {"y": 4, "z": 8, "x": 4, "core": 2}
AXES = ("y", "z", "x", "core")
SHIFT = 1.25
AMPLIFY_MAX = 4.0
GRAM = 2

TILES_PARAMS = pltpu.CompilerParams(vmem_limit_bytes=12 * 1024 * 1024)
SMALL_PARAMS = pltpu.CompilerParams(vmem_limit_bytes=4 * 1024 * 1024)

VMEM = pl.BlockSpec(memory_space=pltpu.VMEM)
SMEM = pl.BlockSpec(memory_space=pltpu.SMEM)
ANY = pl.BlockSpec(memory_space=pl.ANY)


def dot(left, right):
    return lax.dot_general(
        left, right, (((1,), (0,)), ((), ())), precision=HIGH, preferred_element_type=jnp.float32
    )


def dot_t(left, right):
    return lax.dot_general(
        left, right, (((1,), (1,)), ((), ())), precision=HIGH, preferred_element_type=jnp.float32
    )


def struct(shape, dtype):
    return jax.ShapeDtypeStruct(shape, dtype)


def put_gram(out_ref, gram):
    high = gram.astype(jnp.bfloat16)
    out_ref[0] = high
    out_ref[1] = (gram - high.astype(jnp.float32)).astype(jnp.bfloat16)


def get_gram(ref):
    return ref[0].astype(jnp.float32) + ref[1].astype(jnp.float32)


def put_block(out_ref, block):
    for half in range(2):
        out_ref[GRAM + half] = block[:, half * 128 : (half + 1) * 128].astype(jnp.bfloat16)


def first_kernel(start_ref, out_ref):
    block = start_ref[...]
    gram = dot_t(block, block) * (1.0 / NODES)
    put_gram(out_ref, jnp.concatenate([gram, jnp.zeros_like(gram)], axis=1))
    put_block(out_ref, block)


def merge_kernel(a_ref, b_ref, c_ref, d_ref, out_ref):
    refs = (a_ref, b_ref, c_ref, d_ref)
    count = a_ref.shape[0] - GRAM
    put_gram(
        out_ref, (get_gram(a_ref) + get_gram(b_ref)) + (get_gram(c_ref) + get_gram(d_ref))
    )
    for place, ref in enumerate(refs):
        out_ref[GRAM + place * count : GRAM + (place + 1) * count] = ref[GRAM:]


def merge(parts):
    count = parts[0].shape[0] - GRAM
    return pl.pallas_call(
        merge_kernel,
        out_shape=struct((GRAM + 4 * count, K, 128), jnp.bfloat16),
        in_specs=[VMEM] * 4,
        out_specs=VMEM,
        compiler_params=SMALL_PARAMS,
    )(*parts)


def swap(value, axis, mask):
    size = SIZES[axis]
    return lax.ppermute(value, axis, [(i, i ^ mask) for i in range(size)])


def send(value, place_of):
    pairs = []
    for y in range(4):
        for z in range(8):
            for x in range(4):
                to_y, to_z, to_x = place_of(y, z, x)
                pairs.append(((y * 8 + z) * 4 + x, (to_y * 8 + to_z) * 4 + to_x))
    return lax.ppermute(value, ("y", "z", "x"), pairs)


def far_z(z):
    return (z + 8 + 2 * (z % 2) - 1) % 8


def gather(packed):
    packed = merge([packed] + [swap(packed, "z", mask) for mask in (2, 4, 6)])
    near = merge(
        [packed]
        + [
            send(packed, lambda y, z, x: (y, z, x ^ 2)),
            send(packed, lambda y, z, x: (y ^ 2, z, x)),
            send(packed, lambda y, z, x: (y ^ 2, z, x ^ 2)),
        ]
    )
    corner = send(near, lambda y, z, x: (y ^ 3, far_z(z), x ^ 3))
    return [
        near,
        send(near, lambda y, z, x: (y, z, x ^ 1)),
        send(near, lambda y, z, x: (y ^ 1, z, x)),
        send(near, lambda y, z, x: (y, z ^ 1, x)),
        corner,
        send(corner, lambda y, z, x: (y, z, x ^ 3)),
        send(corner, lambda y, z, x: (y ^ 3, z, x)),
        send(corner, lambda y, z, x: (y, far_z(z), x)),
    ]


PIECE = GRAM + 32
BUFFER_OF = (0, 1, 2, 7, 3, 6, 5, 4)


def block_index(cols, y, z, x):
    owner = cols // 2
    ys, zs, xs = owner // 32, owner // 4 % 8, owner % 4
    odd_x, odd_y, odd_z = (xs ^ x) & 1, (ys ^ y) & 1, (zs ^ z) & 1
    buffer = jnp.zeros_like(owner)
    for parity, number in enumerate(BUFFER_OF):
        buffer = jnp.where(odd_x + 2 * odd_y + 4 * odd_z == parity, number, buffer)
    corner = buffer >= 4
    base_x = x ^ jnp.where(corner, 3 * odd_x, odd_x)
    base_y = y ^ jnp.where(corner, 3 * odd_y, odd_y)
    base_z = jnp.where(odd_z == 0, z, jnp.where(corner, far_z(z), z ^ 1))
    index = ((ys >> 1) ^ (base_y >> 1)) * 8 + ((xs >> 1) ^ (base_x >> 1)) * 4 + ((zs >> 1) ^ (base_z >> 1))
    return buffer // 4, buffer % 4 * PIECE + GRAM + index * 2 + cols % 2


DEEP = 4
UNROLL = 8
GROUPS = (SLOTS + 4 * (DEEP - 1) + DEEP * UNROLL - 1) // (DEEP * UNROLL) * UNROLL
ZERO = 4 * PIECE


def slot_list(rows, blocks, live, core):
    slots = jnp.arange(SLOTS, dtype=jnp.int32)
    rows = jnp.where(live, rows, 4)
    earlier = (rows[None, :] == rows[:, None]) & (slots[None, :] < slots[:, None])
    rank = jnp.sum(earlier.astype(jnp.int32), axis=1)
    counts = jnp.sum((rows[None, :] == jnp.arange(4, dtype=jnp.int32)[:, None]).astype(jnp.int32), axis=1)
    ends = jnp.sum(
        jnp.where(
            jnp.arange(4)[None, :] <= jnp.arange(4)[:, None], ((counts + DEEP - 1) // DEEP * DEEP)[None, :], 0
        ),
        axis=1,
    )
    start = jnp.zeros_like(rows)
    for row in range(1, 4):
        start = jnp.where(rows == row, ends[row - 1], start)
    place = jnp.where(rows < 4, start + rank, -1)
    hit = place[None, :] == jnp.arange(DEEP * GROUPS, dtype=jnp.int32)[:, None]
    codes = jnp.sum(jnp.where(hit, (slots * 1024 + blocks - ZERO)[None, :], 0), axis=1) + ZERO
    begin = DEEP * jnp.arange(GROUPS, dtype=jnp.int32)
    product_rows = jnp.sum((begin[:, None] >= ends[None, :]).astype(jnp.int32), axis=1)
    return jnp.concatenate([codes, product_rows, jnp.stack([ends[3], core])]).astype(jnp.int32)


def hold_kernel(tiles_ref, out_ref, sem):
    copy = pltpu.make_async_copy(tiles_ref, out_ref, sem)
    copy.start()
    copy.wait()


def hold_tiles(tiles):
    return pl.pallas_call(
        hold_kernel,
        out_shape=struct(tiles.shape, tiles.dtype),
        in_specs=[ANY],
        out_specs=VMEM,
        scratch_shapes=[pltpu.SemaphoreType.DMA(())],
        compiler_params=TILES_PARAMS,
        cost_estimate=pl.CostEstimate(flops=0, bytes_accessed=16 * 1024 * 1024, transcendentals=0),
    )(tiles)


def add_products(list_ref, tiles_ref, held, sums):
    def products(step, carry):
        results = []
        for u in range(UNROLL):
            base = (step * UNROLL + u) * DEEP
            codes = [list_ref[base + v] for v in range(DEEP)]
            results.append(
                lax.dot_general(
                    jnp.concatenate([held[code & 1023] for code in codes], axis=1),
                    jnp.concatenate([tiles_ref[code >> 10] for code in codes], axis=1),
                    (((1,), (1,)), ((), ())),
                    preferred_element_type=jnp.float32,
                )
            )
        for u in range(UNROLL):
            row = list_ref[DEEP * GROUPS + step * UNROLL + u]
            sums[row] = sums[row] + results[u]
        return carry

    used = list_ref[(DEEP + 1) * GROUPS]
    lax.fori_loop(0, lax.div(used + DEEP * UNROLL - 1, DEEP * UNROLL), products, 0)


def copy_pieces(pieces, held, sems):
    return [
        pltpu.make_async_copy(piece, held.at[pl.ds(number * PIECE, PIECE)], sems.at[number])
        for number, piece in enumerate(pieces)
    ]


def near_kernel(list_ref, tiles_ref, *refs):
    pieces, (sums, held, sems) = refs[:4], refs[4:]
    copies = copy_pieces(pieces, held, sems)
    for copy in copies:
        copy.start()
    held[ZERO] = jnp.zeros((K, 128), jnp.bfloat16)
    sums[...] = jnp.zeros_like(sums)
    for copy in copies:
        copy.wait()
    add_products(list_ref, tiles_ref, held, sums)


def corner_kernel(list_ref, tiles_ref, before_ref, *refs):
    near, pieces = refs[:4], refs[4:8]
    own_ref, other_ref, held, sums, heads, sems, head_sems = refs[8:]
    copies = copy_pieces(pieces, held, sems) + [
        pltpu.make_async_copy(
            piece.at[pl.ds(0, GRAM)], heads.at[pl.ds(number * GRAM, GRAM)], head_sems.at[number]
        )
        for number, piece in enumerate(near)
    ]
    for copy in copies:
        copy.start()
    held[ZERO] = jnp.zeros((K, 128), jnp.bfloat16)
    sums[...] = before_ref[...]
    for copy in copies:
        copy.wait()
    grams = [
        get_gram(heads.at[pl.ds(number * GRAM, GRAM)])
        + get_gram(held.at[pl.ds(number * PIECE, GRAM)])
        for number in range(4)
    ]
    gram = (grams[0] + grams[1]) + (grams[2] + grams[3])
    own_ref[:, 256:] = gram
    other_ref[:, 256:] = gram
    add_products(list_ref, tiles_ref, held, sums)
    core = list_ref[(DEEP + 1) * GROUPS + 1]
    for half in range(2):
        cols = slice(half * 128, (half + 1) * 128)
        own_ref[:, cols] = sums[2 * core + half]
        other_ref[:, cols] = sums[2 * (1 - core) + half]


def tiles_product(slots, tiles, pieces):
    near, corner = pieces[:4], pieces[4:]
    cost = pl.CostEstimate(flops=2 * K * 128 * 128 * SLOTS, bytes_accessed=16 * 1024 * 1024, transcendentals=0)
    blocks = pltpu.VMEM((ZERO + 1, K, 128), jnp.bfloat16)
    sums = pl.pallas_call(
        near_kernel,
        out_shape=struct((5, K, 128), jnp.float32),
        in_specs=[SMEM, VMEM] + [ANY] * 4,
        out_specs=VMEM,
        scratch_shapes=[blocks, pltpu.SemaphoreType.DMA((4,))],
        compiler_params=TILES_PARAMS,
        cost_estimate=cost,
    )(slots[0], tiles, *near)
    return pl.pallas_call(
        corner_kernel,
        out_shape=[struct((K, 384), jnp.float32)] * 2,
        in_specs=[SMEM, VMEM, VMEM] + [ANY] * 8,
        out_specs=[VMEM] * 2,
        scratch_shapes=[
            blocks,
            pltpu.VMEM((5, K, 128), jnp.float32),
            pltpu.VMEM((4 * GRAM, K, 128), jnp.bfloat16),
            pltpu.SemaphoreType.DMA((4,)),
            pltpu.SemaphoreType.DMA((4,)),
        ],
        compiler_params=TILES_PARAMS,
        cost_estimate=cost,
    )(slots[1], tiles, sums, *near, *corner)


def eliminate(gram, held):
    eye = (
        lax.broadcasted_iota(jnp.int32, (K, K), 0) == lax.broadcasted_iota(jnp.int32, (K, K), 1)
    ).astype(jnp.float32)
    whole = jnp.concatenate([gram, eye], axis=1)
    work = [whole[8 * i : 8 * i + 8] for i in range(8)]
    for j in range(0, K, 4):
        first, offset = j // 8, j % 8
        rows = [work[first][offset + u : offset + u + 1] for u in range(4)]
        heads = [
            [jnp.broadcast_to(rows[u][:, j + v : j + v + 1], (1, 128)) for v in range(4)]
            for u in range(4)
        ]
        later = range(first if offset == 0 else first + 1, 8)
        columns = [
            {i: jnp.broadcast_to(work[i][:, j + u : j + u + 1], (8, 128)) for i in later}
            for u in range(4)
        ]
        scaled = []
        for u in range(4):
            over = 1.0 / heads[u][u]
            for v in range(u + 1, 4):
                part = heads[u][v] * over
                rows[v] = rows[v] - part * rows[u]
                for w in range(v, 4):
                    heads[v][w] = heads[v][w] - part * heads[u][w]
                for i in later:
                    columns[v][i] = columns[v][i] - part * columns[u][i]
            scaled.append(rows[u] * over)
        for i in later:
            work[i] = work[i] - (
                (columns[0][i] * scaled[0] + columns[1][i] * scaled[1])
                + (columns[2][i] * scaled[2] + columns[3][i] * scaled[3])
            )
        for u in range(4):
            held[j + u : j + u + 1] = rows[u] * lax.rsqrt(heads[u][u])


def factorize(both, spread_ref, held):
    square, cross = both[:, :K], both[:, K:]
    eliminate(square - dot_t(cross, cross), held)
    result = held[...]
    down = lax.broadcasted_iota(jnp.int32, (K, K), 0)
    right = lax.broadcasted_iota(jnp.int32, (K, K), 1)
    eye = (down == right).astype(jnp.float32)
    upper = jnp.where(right >= down, result[:, :K], 0.0)
    inverse = jnp.where(right <= down, result[:, K:], 0.0)
    carried = dot(inverse, cross)
    record = jnp.concatenate([cross + SHIFT * eye, upper.T], axis=1)
    diagonal = jnp.sum(square * eye, axis=1, keepdims=True)
    spread = dot(inverse * inverse, jnp.broadcast_to(diagonal, (K, 128))) + dot(
        carried * carried, spread_ref[0]
    )
    good = jnp.where(spread < AMPLIFY_MAX, spread_ref[1], 0.0)
    return upper, inverse, carried, record, spread, good


def step_kernel(first, last, own_ref, other_ref, spread_ref, degrees_ref, block_ref, *refs):
    if not first:
        basis_ref, product_ref = refs[:2]
        refs = refs[2:]
    new_block_ref, new_basis_ref, new_product_ref, record_ref, spread_out_ref, packed_ref, held = refs
    both = own_ref[...] + other_ref[...]
    upper, inverse, carried, record, spread, good = factorize(both[:, 256:], spread_ref, held)
    record_ref[...] = record
    spread_out_ref[0] = spread
    spread_out_ref[1] = good
    new_basis = dot(inverse, block_ref[...])
    new_product = dot(inverse, both[:, :256])
    if not first:
        new_basis = new_basis - dot(carried, basis_ref[...])
        new_product = new_product - dot(carried, product_ref[...])
    block = (degrees_ref[...] - SHIFT) * new_basis - new_product
    if not first:
        block = block - dot(upper, basis_ref[...])
    new_block_ref[...] = block
    new_basis_ref[...] = new_basis
    new_product_ref[...] = new_product
    gram = dot_t(block, jnp.concatenate([block, new_basis], axis=0)) * (1.0 / NODES)
    if last:
        packed_ref[...] = gram
    else:
        put_gram(packed_ref, gram)
        put_block(packed_ref, block)


def step(last, own, other, spread, degrees, block, *earlier):
    wide = struct((K, 256), jnp.float32)
    return pl.pallas_call(
        functools.partial(step_kernel, not earlier, last),
        out_shape=[
            wide,
            wide,
            wide,
            struct((K, 128), jnp.float32),
            struct((2, K, 128), jnp.float32),
            struct((K, 128), jnp.float32) if last else struct((GRAM + 2, K, 128), jnp.bfloat16),
        ],
        in_specs=[VMEM] * (5 + len(earlier)),
        out_specs=[VMEM] * 6,
        scratch_shapes=[pltpu.VMEM((K, 128), jnp.float32)],
        compiler_params=SMALL_PARAMS,
    )(own, other, spread, degrees, block, *earlier)


def last_kernel(
    own_ref, other_ref, spread_ref, block_ref, basis_ref, first_ref, second_ref,
    out_ref, records_ref, good_ref, held,
):
    _, inverse, carried, record, _, good = factorize(own_ref[...] + other_ref[...], spread_ref, held)
    out_ref[...] = dot(inverse, block_ref[...]) - dot(carried, basis_ref[...])
    records_ref[0] = first_ref[...]
    records_ref[1] = second_ref[...]
    records_ref[2] = record
    good_ref[0, 0] = jnp.min(good)


def total_over_devices(value):
    for axis, masks in (("x", (1, 2, 3)), ("y", (1, 2, 3)), ("z", (2, 4, 6)), ("z", (1,))):
        parts = [value] + [swap(value, axis, mask) for mask in masks]
        value = parts[0] + parts[1]
        if len(parts) == 4:
            value = value + (parts[2] + parts[3])
    return value


def short_path(tiles, tile_rows, tile_cols, tile_counts, degrees, start_block):
    y, z, x, core = (lax.axis_index(axis) for axis in AXES)
    live = tile_counts.reshape(())
    tile_set = hold_tiles(tiles.reshape(SLOTS, 128, 128))
    half, blocks = block_index(tile_cols.reshape(-1), y, z, x)
    alive = jnp.arange(SLOTS, dtype=jnp.int32) < live
    slots = [
        slot_list(tile_rows.reshape(-1), blocks, alive & (half == number), core) for number in range(2)
    ]
    degrees = degrees.reshape(1, -1)

    packed = pl.pallas_call(
        first_kernel,
        out_shape=struct((GRAM + 2, K, 128), jnp.bfloat16),
        in_specs=[VMEM],
        out_specs=VMEM,
        compiler_params=SMALL_PARAMS,
    )(start_block)
    block = start_block
    earlier = ()
    spread = jnp.stack([jnp.zeros((K, 128), jnp.float32), jnp.ones((K, 128), jnp.float32)])
    records = []
    for sweep in range(ITERS):
        own, other = tiles_product(slots, tile_set, gather(packed))
        block, basis, product, record, spread, packed = step(
            sweep == ITERS - 1, own, swap(other, "core", 1), spread, degrees, block, *earlier
        )
        earlier = (basis, product)
        records.append(record)
    gram = total_over_devices(packed)
    basis, records, good = pl.pallas_call(
        last_kernel,
        out_shape=[
            struct((K, 256), jnp.float32),
            struct((ITERS, K, 128), jnp.float32),
            struct((1, 1), jnp.float32),
        ],
        in_specs=[VMEM] * 7,
        out_specs=[VMEM, VMEM, SMEM],
        compiler_params=SMALL_PARAMS,
        scratch_shapes=[pltpu.VMEM((K, 128), jnp.float32)],
    )(gram, swap(gram, "core", 1), spread, block, basis, records[1], records[2])
    return basis, records, good[0, 0]


def tile_terms(totals, blocks, tile_set, row_ids, col_ids, live_count, step_size):
    slab_rows = totals.shape[1]

    def one_block(block_id, running):
        offset = block_id * step_size
        part_tiles = lax.dynamic_slice_in_dim(tile_set, offset, step_size, 0)
        part_rows = lax.dynamic_slice_in_dim(row_ids, offset, step_size, 0)
        part_cols = lax.dynamic_slice_in_dim(col_ids, offset, step_size, 0)
        slot_ids = offset + jnp.arange(step_size, dtype=jnp.int32)
        columns = jnp.take(blocks, part_cols, axis=1)
        contrib = jnp.einsum(
            "ktj,tij->tki", columns, part_tiles, preferred_element_type=jnp.float32
        )
        onehot = (
            (part_rows[:, None] == jnp.arange(slab_rows, dtype=jnp.int32)[None, :])
            & (slot_ids < live_count)[:, None]
        ).astype(jnp.float32)
        return running + jnp.einsum("tr,tki->kri", onehot, contrib, precision=HIGH)

    return lax.fori_loop(0, tile_set.shape[0] // step_size, one_block, totals)


def plain_factorize(block, gram_matrix):
    factor_low = jnp.linalg.cholesky(gram_matrix)
    new_basis = jax.scipy.linalg.solve_triangular(factor_low, block, lower=True)
    return (new_basis, factor_low)


def plain_path(tiles, tile_rows, tile_cols, tile_counts, degrees, start_block):
    vectors = start_block.shape[0]
    own_cols = start_block.shape[1]
    slab_rows = 2 * (own_cols // 128)
    tile_set = tiles.reshape(tiles.shape[2], 128, 128)
    row_ids = tile_rows.reshape(-1)
    col_ids = tile_cols.reshape(-1)
    live_count = tile_counts.reshape(())

    def gram_of(left, right):
        return lax.psum(jnp.dot(left, right.T, precision=HIGH), AXES) / NODES

    basis, factor_low = plain_factorize(start_block, gram_of(start_block, start_block))
    previous = jnp.zeros_like(basis)
    coupling = jnp.zeros((vectors, vectors), jnp.float32)
    records = []
    for sweep in range(ITERS):
        blocks = lax.all_gather(
            basis.astype(jnp.bfloat16), ("y", "z", "x"), axis=1, tiled=True
        ).reshape(vectors, -1, 128)
        totals = jnp.zeros((vectors, slab_rows, 128), jnp.float32)
        totals = tile_terms(totals, blocks, tile_set, row_ids, col_ids, live_count, 32)
        product = lax.psum_scatter(
            totals.reshape(vectors, slab_rows * 128), "core", scatter_dimension=1, tiled=True
        )
        image_block = degrees[None, :] * basis - product
        diag_block = gram_of(image_block, basis)
        residual = (
            image_block
            - jnp.dot(diag_block, basis, precision=HIGH)
            - jnp.dot(coupling, previous, precision=HIGH)
        )
        new_basis, factor_low = plain_factorize(residual, gram_of(residual, residual))
        records.append(jnp.concatenate([diag_block, factor_low], axis=1))
        previous, basis, coupling = (basis, new_basis, factor_low.T)
    return (basis, jnp.stack(records))


def body(*args):
    basis, records, good = short_path(*args)
    return lax.cond(good > 0.5, lambda *rest: (basis, records), plain_path, *args)


def solution(mesh):
    split = Mesh(mesh.devices.reshape(tuple(SIZES[axis] for axis in AXES)), AXES)
    row = ("y", "z", "x")
    in_specs = (
        P(row, "core", None, None, None),
        P(row, "core", None),
        P(row, "core", None),
        P(row, "core"),
        P(AXES),
        P(None, AXES),
    )
    out_specs = (P(None, AXES), P())
    return jax.shard_map(body, mesh=split, in_specs=in_specs, out_specs=out_specs, check_vma=False)
```

```python
import functools

import jax
import jax.numpy as jnp
from jax import lax
from jax.experimental import pallas as pl
from jax.experimental.pallas import tpu as pltpu
from jax.sharding import Mesh, PartitionSpec as P

ITERS = 3
HIGH = lax.Precision.HIGHEST

K = 64
SLOTS = 256
NODES = 65536
SIZES = {"y": 4, "z": 8, "x": 4, "core": 2}
AXES = ("y", "z", "x", "core")
SHIFT = 1.25
AMPLIFY_MAX = 4.0
GRAM = 2

TILES_PARAMS = pltpu.CompilerParams(vmem_limit_bytes=12 * 1024 * 1024)
SMALL_PARAMS = pltpu.CompilerParams(vmem_limit_bytes=4 * 1024 * 1024)

VMEM = pl.BlockSpec(memory_space=pltpu.VMEM)
SMEM = pl.BlockSpec(memory_space=pltpu.SMEM)
ANY = pl.BlockSpec(memory_space=pl.ANY)


def dot(left, right):
    return lax.dot_general(
        left, right, (((1,), (0,)), ((), ())), precision=HIGH, preferred_element_type=jnp.float32
    )


def dot_t(left, right):
    return lax.dot_general(
        left, right, (((1,), (1,)), ((), ())), precision=HIGH, preferred_element_type=jnp.float32
    )


def struct(shape, dtype):
    return jax.ShapeDtypeStruct(shape, dtype)


def put_gram(out_ref, gram):
    high = gram.astype(jnp.bfloat16)
    out_ref[0] = high
    out_ref[1] = (gram - high.astype(jnp.float32)).astype(jnp.bfloat16)


def get_gram(ref):
    return ref[0].astype(jnp.float32) + ref[1].astype(jnp.float32)


def put_block(out_ref, block):
    for half in range(2):
        out_ref[GRAM + half] = block[:, half * 128 : (half + 1) * 128].astype(jnp.bfloat16)


def first_kernel(start_ref, out_ref):
    block = start_ref[...]
    gram = dot_t(block, block) * (1.0 / NODES)
    put_gram(out_ref, jnp.concatenate([gram, jnp.zeros_like(gram)], axis=1))
    put_block(out_ref, block)


def merge_kernel(a_ref, b_ref, c_ref, d_ref, out_ref):
    refs = (a_ref, b_ref, c_ref, d_ref)
    count = a_ref.shape[0] - GRAM
    put_gram(
        out_ref, (get_gram(a_ref) + get_gram(b_ref)) + (get_gram(c_ref) + get_gram(d_ref))
    )
    for place, ref in enumerate(refs):
        out_ref[GRAM + place * count : GRAM + (place + 1) * count] = ref[GRAM:]


def merge(parts):
    count = parts[0].shape[0] - GRAM
    return pl.pallas_call(
        merge_kernel,
        out_shape=struct((GRAM + 4 * count, K, 128), jnp.bfloat16),
        in_specs=[VMEM] * 4,
        out_specs=VMEM,
        compiler_params=SMALL_PARAMS,
    )(*parts)


def swap(value, axis, mask):
    size = SIZES[axis]
    return lax.ppermute(value, axis, [(i, i ^ mask) for i in range(size)])


def send(value, place_of):
    pairs = []
    for y in range(4):
        for z in range(8):
            for x in range(4):
                to_y, to_z, to_x = place_of(y, z, x)
                pairs.append(((y * 8 + z) * 4 + x, (to_y * 8 + to_z) * 4 + to_x))
    return lax.ppermute(value, ("y", "z", "x"), pairs)


def far_z(z):
    return (z + 8 + 2 * (z % 2) - 1) % 8


def gather(packed):
    packed = merge([packed] + [swap(packed, "z", mask) for mask in (2, 4, 6)])
    near = merge(
        [packed]
        + [
            send(packed, lambda y, z, x: (y, z, x ^ 2)),
            send(packed, lambda y, z, x: (y ^ 2, z, x)),
            send(packed, lambda y, z, x: (y ^ 2, z, x ^ 2)),
        ]
    )
    near_x = send(near, lambda y, z, x: (y, z, x ^ 1))
    near_y = send(near, lambda y, z, x: (y ^ 1, z, x))
    near_z = send(near, lambda y, z, x: (y, z ^ 1, x))
    return [
        near,
        near_x,
        near_y,
        near_z,
        send(near, lambda y, z, x: (y ^ 3, far_z(z), x ^ 3)),
        send(near_z, lambda y, z, x: (y ^ 1, z, x)),
        send(near_x, lambda y, z, x: (y, z ^ 1, x)),
        send(near_y, lambda y, z, x: (y, z, x ^ 1)),
    ]


PIECE = GRAM + 32
BUFFER_OF = (0, 1, 2, 7, 3, 6, 5, 4)


def block_index(cols, y, z, x):
    owner = cols // 2
    ys, zs, xs = owner // 32, owner // 4 % 8, owner % 4
    odd_x, odd_y, odd_z = (xs ^ x) & 1, (ys ^ y) & 1, (zs ^ z) & 1
    buffer = jnp.zeros_like(owner)
    for parity, number in enumerate(BUFFER_OF):
        buffer = jnp.where(odd_x + 2 * odd_y + 4 * odd_z == parity, number, buffer)
    corner = buffer == 4
    base_x = x ^ jnp.where(corner, 3 * odd_x, odd_x)
    base_y = y ^ jnp.where(corner, 3 * odd_y, odd_y)
    base_z = jnp.where(odd_z == 0, z, jnp.where(corner, far_z(z), z ^ 1))
    index = ((ys >> 1) ^ (base_y >> 1)) * 8 + ((xs >> 1) ^ (base_x >> 1)) * 4 + ((zs >> 1) ^ (base_z >> 1))
    return buffer // 4, buffer % 4 * PIECE + GRAM + index * 2 + cols % 2


DEEP = 4
UNROLL = 8
GROUPS = (SLOTS + 4 * (DEEP - 1) + DEEP * UNROLL - 1) // (DEEP * UNROLL) * UNROLL
ZERO = 4 * PIECE


def slot_list(rows, blocks, live, core):
    slots = jnp.arange(SLOTS, dtype=jnp.int32)
    rows = jnp.where(live, rows, 4)
    earlier = (rows[None, :] == rows[:, None]) & (slots[None, :] < slots[:, None])
    rank = jnp.sum(earlier.astype(jnp.int32), axis=1)
    counts = jnp.sum((rows[None, :] == jnp.arange(4, dtype=jnp.int32)[:, None]).astype(jnp.int32), axis=1)
    ends = jnp.sum(
        jnp.where(
            jnp.arange(4)[None, :] <= jnp.arange(4)[:, None], ((counts + DEEP - 1) // DEEP * DEEP)[None, :], 0
        ),
        axis=1,
    )
    start = jnp.zeros_like(rows)
    for row in range(1, 4):
        start = jnp.where(rows == row, ends[row - 1], start)
    place = jnp.where(rows < 4, start + rank, -1)
    hit = place[None, :] == jnp.arange(DEEP * GROUPS, dtype=jnp.int32)[:, None]
    codes = jnp.sum(jnp.where(hit, (slots * 1024 + blocks - ZERO)[None, :], 0), axis=1) + ZERO
    begin = DEEP * jnp.arange(GROUPS, dtype=jnp.int32)
    product_rows = jnp.sum((begin[:, None] >= ends[None, :]).astype(jnp.int32), axis=1)
    return jnp.concatenate([codes, product_rows, jnp.stack([ends[3], core])]).astype(jnp.int32)


def hold_kernel(tiles_ref, out_ref, sem):
    copy = pltpu.make_async_copy(tiles_ref, out_ref, sem)
    copy.start()
    copy.wait()


def hold_tiles(tiles):
    return pl.pallas_call(
        hold_kernel,
        out_shape=struct(tiles.shape, tiles.dtype),
        in_specs=[ANY],
        out_specs=VMEM,
        scratch_shapes=[pltpu.SemaphoreType.DMA(())],
        compiler_params=TILES_PARAMS,
        cost_estimate=pl.CostEstimate(flops=0, bytes_accessed=16 * 1024 * 1024, transcendentals=0),
    )(tiles)


def add_products(list_ref, tiles_ref, held, sums):
    def products(step, carry):
        results = []
        for u in range(UNROLL):
            base = (step * UNROLL + u) * DEEP
            codes = [list_ref[base + v] for v in range(DEEP)]
            results.append(
                lax.dot_general(
                    jnp.concatenate([held[code & 1023] for code in codes], axis=1),
                    jnp.concatenate([tiles_ref[code >> 10] for code in codes], axis=1),
                    (((1,), (1,)), ((), ())),
                    preferred_element_type=jnp.float32,
                )
            )
        for u in range(UNROLL):
            row = list_ref[DEEP * GROUPS + step * UNROLL + u]
            sums[row] = sums[row] + results[u]
        return carry

    used = list_ref[(DEEP + 1) * GROUPS]
    lax.fori_loop(0, lax.div(used + DEEP * UNROLL - 1, DEEP * UNROLL), products, 0)


def copy_pieces(pieces, held, sems):
    return [
        pltpu.make_async_copy(piece, held.at[pl.ds(number * PIECE, PIECE)], sems.at[number])
        for number, piece in enumerate(pieces)
    ]


def near_kernel(list_ref, tiles_ref, *refs):
    pieces, (sums, held, sems) = refs[:4], refs[4:]
    copies = copy_pieces(pieces, held, sems)
    for copy in copies:
        copy.start()
    held[ZERO] = jnp.zeros((K, 128), jnp.bfloat16)
    sums[...] = jnp.zeros_like(sums)
    for copy in copies:
        copy.wait()
    add_products(list_ref, tiles_ref, held, sums)


def corner_kernel(list_ref, tiles_ref, before_ref, *refs):
    near, pieces = refs[:4], refs[4:8]
    own_ref, other_ref, held, sums, heads, sems, head_sems = refs[8:]
    copies = copy_pieces(pieces, held, sems) + [
        pltpu.make_async_copy(
            piece.at[pl.ds(0, GRAM)], heads.at[pl.ds(number * GRAM, GRAM)], head_sems.at[number]
        )
        for number, piece in enumerate(near)
    ]
    for copy in copies:
        copy.start()
    held[ZERO] = jnp.zeros((K, 128), jnp.bfloat16)
    sums[...] = before_ref[...]
    for copy in copies:
        copy.wait()
    grams = [
        get_gram(heads.at[pl.ds(number * GRAM, GRAM)])
        + get_gram(held.at[pl.ds(number * PIECE, GRAM)])
        for number in range(4)
    ]
    gram = (grams[0] + grams[1]) + (grams[2] + grams[3])
    own_ref[:, 256:] = gram
    other_ref[:, 256:] = gram
    add_products(list_ref, tiles_ref, held, sums)
    core = list_ref[(DEEP + 1) * GROUPS + 1]
    for half in range(2):
        cols = slice(half * 128, (half + 1) * 128)
        own_ref[:, cols] = sums[2 * core + half]
        other_ref[:, cols] = sums[2 * (1 - core) + half]


def tiles_product(slots, tiles, pieces):
    near, corner = pieces[:4], pieces[4:]
    cost = pl.CostEstimate(flops=2 * K * 128 * 128 * SLOTS, bytes_accessed=16 * 1024 * 1024, transcendentals=0)
    blocks = pltpu.VMEM((ZERO + 1, K, 128), jnp.bfloat16)
    sums = pl.pallas_call(
        near_kernel,
        out_shape=struct((5, K, 128), jnp.float32),
        in_specs=[SMEM, VMEM] + [ANY] * 4,
        out_specs=VMEM,
        scratch_shapes=[blocks, pltpu.SemaphoreType.DMA((4,))],
        compiler_params=TILES_PARAMS,
        cost_estimate=cost,
    )(slots[0], tiles, *near)
    return pl.pallas_call(
        corner_kernel,
        out_shape=[struct((K, 384), jnp.float32)] * 2,
        in_specs=[SMEM, VMEM, VMEM] + [ANY] * 8,
        out_specs=[VMEM] * 2,
        scratch_shapes=[
            blocks,
            pltpu.VMEM((5, K, 128), jnp.float32),
            pltpu.VMEM((4 * GRAM, K, 128), jnp.bfloat16),
            pltpu.SemaphoreType.DMA((4,)),
            pltpu.SemaphoreType.DMA((4,)),
        ],
        compiler_params=TILES_PARAMS,
        cost_estimate=cost,
    )(slots[1], tiles, sums, *near, *corner)


def eliminate(gram, held):
    eye = (
        lax.broadcasted_iota(jnp.int32, (K, K), 0) == lax.broadcasted_iota(jnp.int32, (K, K), 1)
    ).astype(jnp.float32)
    whole = jnp.concatenate([gram, eye], axis=1)
    work = [whole[8 * i : 8 * i + 8] for i in range(8)]
    for j in range(0, K, 4):
        first, offset = j // 8, j % 8
        rows = [work[first][offset + u : offset + u + 1] for u in range(4)]
        heads = [
            [jnp.broadcast_to(rows[u][:, j + v : j + v + 1], (1, 128)) for v in range(4)]
            for u in range(4)
        ]
        later = range(first if offset == 0 else first + 1, 8)
        columns = [
            {i: jnp.broadcast_to(work[i][:, j + u : j + u + 1], (8, 128)) for i in later}
            for u in range(4)
        ]
        scaled = []
        for u in range(4):
            over = 1.0 / heads[u][u]
            for v in range(u + 1, 4):
                part = heads[u][v] * over
                rows[v] = rows[v] - part * rows[u]
                for w in range(v, 4):
                    heads[v][w] = heads[v][w] - part * heads[u][w]
                for i in later:
                    columns[v][i] = columns[v][i] - part * columns[u][i]
            scaled.append(rows[u] * over)
        for i in later:
            work[i] = work[i] - (
                (columns[0][i] * scaled[0] + columns[1][i] * scaled[1])
                + (columns[2][i] * scaled[2] + columns[3][i] * scaled[3])
            )
        for u in range(4):
            held[j + u : j + u + 1] = rows[u] * lax.rsqrt(heads[u][u])


def factorize(both, spread_ref, held):
    square, cross = both[:, :K], both[:, K:]
    eliminate(square - dot_t(cross, cross), held)
    result = held[...]
    down = lax.broadcasted_iota(jnp.int32, (K, K), 0)
    right = lax.broadcasted_iota(jnp.int32, (K, K), 1)
    eye = (down == right).astype(jnp.float32)
    upper = jnp.where(right >= down, result[:, :K], 0.0)
    inverse = jnp.where(right <= down, result[:, K:], 0.0)
    carried = dot(inverse, cross)
    record = jnp.concatenate([cross + SHIFT * eye, upper.T], axis=1)
    diagonal = jnp.sum(square * eye, axis=1, keepdims=True)
    spread = dot(inverse * inverse, jnp.broadcast_to(diagonal, (K, 128))) + dot(
        carried * carried, spread_ref[0]
    )
    good = jnp.where(spread < AMPLIFY_MAX, spread_ref[1], 0.0)
    return upper, inverse, carried, record, spread, good


def step_kernel(first, last, own_ref, other_ref, spread_ref, degrees_ref, block_ref, *refs):
    if not first:
        basis_ref, product_ref = refs[:2]
        refs = refs[2:]
    new_block_ref, new_basis_ref, new_product_ref, record_ref, spread_out_ref, packed_ref, held = refs
    both = own_ref[...] + other_ref[...]
    upper, inverse, carried, record, spread, good = factorize(both[:, 256:], spread_ref, held)
    record_ref[...] = record
    spread_out_ref[0] = spread
    spread_out_ref[1] = good
    new_basis = dot(inverse, block_ref[...])
    new_product = dot(inverse, both[:, :256])
    if not first:
        new_basis = new_basis - dot(carried, basis_ref[...])
        new_product = new_product - dot(carried, product_ref[...])
    block = (degrees_ref[...] - SHIFT) * new_basis - new_product
    if not first:
        block = block - dot(upper, basis_ref[...])
    new_block_ref[...] = block
    new_basis_ref[...] = new_basis
    new_product_ref[...] = new_product
    gram = dot_t(block, jnp.concatenate([block, new_basis], axis=0)) * (1.0 / NODES)
    if last:
        packed_ref[...] = gram
    else:
        put_gram(packed_ref, gram)
        put_block(packed_ref, block)


def step(last, own, other, spread, degrees, block, *earlier):
    wide = struct((K, 256), jnp.float32)
    return pl.pallas_call(
        functools.partial(step_kernel, not earlier, last),
        out_shape=[
            wide,
            wide,
            wide,
            struct((K, 128), jnp.float32),
            struct((2, K, 128), jnp.float32),
            struct((K, 128), jnp.float32) if last else struct((GRAM + 2, K, 128), jnp.bfloat16),
        ],
        in_specs=[VMEM] * (5 + len(earlier)),
        out_specs=[VMEM] * 6,
        scratch_shapes=[pltpu.VMEM((K, 128), jnp.float32)],
        compiler_params=SMALL_PARAMS,
    )(own, other, spread, degrees, block, *earlier)


def last_kernel(
    own_ref, other_ref, spread_ref, block_ref, basis_ref, first_ref, second_ref,
    out_ref, records_ref, good_ref, held,
):
    _, inverse, carried, record, _, good = factorize(own_ref[...] + other_ref[...], spread_ref, held)
    out_ref[...] = dot(inverse, block_ref[...]) - dot(carried, basis_ref[...])
    records_ref[0] = first_ref[...]
    records_ref[1] = second_ref[...]
    records_ref[2] = record
    good_ref[0, 0] = jnp.min(good)


def total_over_devices(value):
    for axis, masks in (("x", (1, 2, 3)), ("y", (1, 2, 3)), ("z", (2, 4, 6)), ("z", (1,))):
        parts = [value] + [swap(value, axis, mask) for mask in masks]
        value = parts[0] + parts[1]
        if len(parts) == 4:
            value = value + (parts[2] + parts[3])
    return value


def short_path(tiles, tile_rows, tile_cols, tile_counts, degrees, start_block):
    y, z, x, core = (lax.axis_index(axis) for axis in AXES)
    live = tile_counts.reshape(())
    tile_set = hold_tiles(tiles.reshape(SLOTS, 128, 128))
    half, blocks = block_index(tile_cols.reshape(-1), y, z, x)
    alive = jnp.arange(SLOTS, dtype=jnp.int32) < live
    slots = [
        slot_list(tile_rows.reshape(-1), blocks, alive & (half == number), core) for number in range(2)
    ]
    degrees = degrees.reshape(1, -1)

    packed = pl.pallas_call(
        first_kernel,
        out_shape=struct((GRAM + 2, K, 128), jnp.bfloat16),
        in_specs=[VMEM],
        out_specs=VMEM,
        compiler_params=SMALL_PARAMS,
    )(start_block)
    block = start_block
    earlier = ()
    spread = jnp.stack([jnp.zeros((K, 128), jnp.float32), jnp.ones((K, 128), jnp.float32)])
    records = []
    for sweep in range(ITERS):
        own, other = tiles_product(slots, tile_set, gather(packed))
        block, basis, product, record, spread, packed = step(
            sweep == ITERS - 1, own, swap(other, "core", 1), spread, degrees, block, *earlier
        )
        earlier = (basis, product)
        records.append(record)
    gram = total_over_devices(packed)
    basis, records, good = pl.pallas_call(
        last_kernel,
        out_shape=[
            struct((K, 256), jnp.float32),
            struct((ITERS, K, 128), jnp.float32),
            struct((1, 1), jnp.float32),
        ],
        in_specs=[VMEM] * 7,
        out_specs=[VMEM, VMEM, SMEM],
        compiler_params=SMALL_PARAMS,
        scratch_shapes=[pltpu.VMEM((K, 128), jnp.float32)],
    )(gram, swap(gram, "core", 1), spread, block, basis, records[1], records[2])
    return basis, records, good[0, 0]


def tile_terms(totals, blocks, tile_set, row_ids, col_ids, live_count, step_size):
    slab_rows = totals.shape[1]

    def one_block(block_id, running):
        offset = block_id * step_size
        part_tiles = lax.dynamic_slice_in_dim(tile_set, offset, step_size, 0)
        part_rows = lax.dynamic_slice_in_dim(row_ids, offset, step_size, 0)
        part_cols = lax.dynamic_slice_in_dim(col_ids, offset, step_size, 0)
        slot_ids = offset + jnp.arange(step_size, dtype=jnp.int32)
        columns = jnp.take(blocks, part_cols, axis=1)
        contrib = jnp.einsum(
            "ktj,tij->tki", columns, part_tiles, preferred_element_type=jnp.float32
        )
        onehot = (
            (part_rows[:, None] == jnp.arange(slab_rows, dtype=jnp.int32)[None, :])
            & (slot_ids < live_count)[:, None]
        ).astype(jnp.float32)
        return running + jnp.einsum("tr,tki->kri", onehot, contrib, precision=HIGH)

    return lax.fori_loop(0, tile_set.shape[0] // step_size, one_block, totals)


def plain_factorize(block, gram_matrix):
    factor_low = jnp.linalg.cholesky(gram_matrix)
    new_basis = jax.scipy.linalg.solve_triangular(factor_low, block, lower=True)
    return (new_basis, factor_low)


def plain_path(tiles, tile_rows, tile_cols, tile_counts, degrees, start_block):
    vectors = start_block.shape[0]
    own_cols = start_block.shape[1]
    slab_rows = 2 * (own_cols // 128)
    tile_set = tiles.reshape(tiles.shape[2], 128, 128)
    row_ids = tile_rows.reshape(-1)
    col_ids = tile_cols.reshape(-1)
    live_count = tile_counts.reshape(())

    def gram_of(left, right):
        return lax.psum(jnp.dot(left, right.T, precision=HIGH), AXES) / NODES

    basis, factor_low = plain_factorize(start_block, gram_of(start_block, start_block))
    previous = jnp.zeros_like(basis)
    coupling = jnp.zeros((vectors, vectors), jnp.float32)
    records = []
    for sweep in range(ITERS):
        blocks = lax.all_gather(
            basis.astype(jnp.bfloat16), ("y", "z", "x"), axis=1, tiled=True
        ).reshape(vectors, -1, 128)
        totals = jnp.zeros((vectors, slab_rows, 128), jnp.float32)
        totals = tile_terms(totals, blocks, tile_set, row_ids, col_ids, live_count, 32)
        product = lax.psum_scatter(
            totals.reshape(vectors, slab_rows * 128), "core", scatter_dimension=1, tiled=True
        )
        image_block = degrees[None, :] * basis - product
        diag_block = gram_of(image_block, basis)
        residual = (
            image_block
            - jnp.dot(diag_block, basis, precision=HIGH)
            - jnp.dot(coupling, previous, precision=HIGH)
        )
        new_basis, factor_low = plain_factorize(residual, gram_of(residual, residual))
        records.append(jnp.concatenate([diag_block, factor_low], axis=1))
        previous, basis, coupling = (basis, new_basis, factor_low.T)
    return (basis, jnp.stack(records))


def body(*args):
    basis, records, good = short_path(*args)
    return lax.cond(good > 0.5, lambda *rest: (basis, records), plain_path, *args)


def solution(mesh):
    split = Mesh(mesh.devices.reshape(tuple(SIZES[axis] for axis in AXES)), AXES)
    row = ("y", "z", "x")
    in_specs = (
        P(row, "core", None, None, None),
        P(row, "core", None),
        P(row, "core", None),
        P(row, "core"),
        P(AXES),
        P(None, AXES),
    )
    out_specs = (P(None, AXES), P())
    return jax.shard_map(body, mesh=split, in_specs=in_specs, out_specs=out_specs, check_vma=False)
```

```python
import functools

import jax
import jax.numpy as jnp
from jax import lax
from jax.experimental import pallas as pl
from jax.experimental.pallas import tpu as pltpu
from jax.sharding import Mesh, PartitionSpec as P

ITERS = 3
HIGH = lax.Precision.HIGHEST

K = 64
SLOTS = 256
NODES = 65536
SIZES = {"y": 4, "z": 8, "x": 4, "core": 2}
AXES = ("y", "z", "x", "core")
SHIFT = 1.25
AMPLIFY_MAX = 4.0
GRAM = 2

TILES_PARAMS = pltpu.CompilerParams(vmem_limit_bytes=12 * 1024 * 1024)
SMALL_PARAMS = pltpu.CompilerParams(vmem_limit_bytes=4 * 1024 * 1024)

VMEM = pl.BlockSpec(memory_space=pltpu.VMEM)
SMEM = pl.BlockSpec(memory_space=pltpu.SMEM)
ANY = pl.BlockSpec(memory_space=pl.ANY)


def dot(left, right):
    return lax.dot_general(
        left, right, (((1,), (0,)), ((), ())), precision=HIGH, preferred_element_type=jnp.float32
    )


def dot_t(left, right):
    return lax.dot_general(
        left, right, (((1,), (1,)), ((), ())), precision=HIGH, preferred_element_type=jnp.float32
    )


def struct(shape, dtype):
    return jax.ShapeDtypeStruct(shape, dtype)


def put_gram(out_ref, gram):
    high = gram.astype(jnp.bfloat16)
    out_ref[0] = high
    out_ref[1] = (gram - high.astype(jnp.float32)).astype(jnp.bfloat16)


def get_gram(ref):
    return ref[0].astype(jnp.float32) + ref[1].astype(jnp.float32)


def put_block(out_ref, block):
    for half in range(2):
        out_ref[GRAM + half] = block[:, half * 128 : (half + 1) * 128].astype(jnp.bfloat16)


def first_kernel(start_ref, out_ref):
    block = start_ref[...]
    gram = dot_t(block, block) * (1.0 / NODES)
    put_gram(out_ref, jnp.concatenate([gram, jnp.zeros_like(gram)], axis=1))
    put_block(out_ref, block)


def merge_kernel(a_ref, b_ref, c_ref, d_ref, out_ref):
    refs = (a_ref, b_ref, c_ref, d_ref)
    count = a_ref.shape[0] - GRAM
    put_gram(
        out_ref, (get_gram(a_ref) + get_gram(b_ref)) + (get_gram(c_ref) + get_gram(d_ref))
    )
    for place, ref in enumerate(refs):
        out_ref[GRAM + place * count : GRAM + (place + 1) * count] = ref[GRAM:]


def merge(parts):
    count = parts[0].shape[0] - GRAM
    return pl.pallas_call(
        merge_kernel,
        out_shape=struct((GRAM + 4 * count, K, 128), jnp.bfloat16),
        in_specs=[VMEM] * 4,
        out_specs=VMEM,
        compiler_params=SMALL_PARAMS,
    )(*parts)


def swap(value, axis, mask):
    size = SIZES[axis]
    return lax.ppermute(value, axis, [(i, i ^ mask) for i in range(size)])


def send(value, place_of):
    pairs = []
    for y in range(4):
        for z in range(8):
            for x in range(4):
                to_y, to_z, to_x = place_of(y, z, x)
                pairs.append(((y * 8 + z) * 4 + x, (to_y * 8 + to_z) * 4 + to_x))
    return lax.ppermute(value, ("y", "z", "x"), pairs)


def far_z(z):
    return (z + 8 + 2 * (z % 2) - 1) % 8


def gather(packed):
    packed = merge([packed] + [swap(packed, "z", mask) for mask in (2, 4, 6)])
    near = merge(
        [packed]
        + [
            send(packed, lambda y, z, x: (y, z, x ^ 2)),
            send(packed, lambda y, z, x: (y ^ 2, z, x)),
            send(packed, lambda y, z, x: (y ^ 2, z, x ^ 2)),
        ]
    )
    near_x = send(near, lambda y, z, x: (y, z, x ^ 1))
    near_y = send(near, lambda y, z, x: (y ^ 1, z, x))
    near_z = send(near, lambda y, z, x: (y, z ^ 1, x))
    return [
        near,
        near_x,
        near_y,
        near_z,
        send(near, lambda y, z, x: (y ^ 3, far_z(z), x ^ 3)),
        send(near_z, lambda y, z, x: (y ^ 1, z, x)),
        send(near_x, lambda y, z, x: (y, z ^ 1, x)),
        send(near_y, lambda y, z, x: (y, z, x ^ 1)),
    ]


PIECE = GRAM + 32
BUFFER_OF = (0, 1, 2, 7, 3, 6, 5, 4)


def block_index(cols, y, z, x):
    owner = cols // 2
    ys, zs, xs = owner // 32, owner // 4 % 8, owner % 4
    odd_x, odd_y, odd_z = (xs ^ x) & 1, (ys ^ y) & 1, (zs ^ z) & 1
    buffer = jnp.zeros_like(owner)
    for parity, number in enumerate(BUFFER_OF):
        buffer = jnp.where(odd_x + 2 * odd_y + 4 * odd_z == parity, number, buffer)
    corner = buffer == 4
    base_x = x ^ jnp.where(corner, 3 * odd_x, odd_x)
    base_y = y ^ jnp.where(corner, 3 * odd_y, odd_y)
    base_z = jnp.where(odd_z == 0, z, jnp.where(corner, far_z(z), z ^ 1))
    index = ((ys >> 1) ^ (base_y >> 1)) * 8 + ((xs >> 1) ^ (base_x >> 1)) * 4 + ((zs >> 1) ^ (base_z >> 1))
    return buffer // 4, buffer % 4 * PIECE + GRAM + index * 2 + cols % 2


DEEP = 4
UNROLL = 8
GROUPS = (SLOTS + 4 * (DEEP - 1) + DEEP * UNROLL - 1) // (DEEP * UNROLL) * UNROLL
ZERO = 4 * PIECE


def slot_list(rows, blocks, live, core):
    slots = jnp.arange(SLOTS, dtype=jnp.int32)
    rows = jnp.where(live, rows, 4)
    earlier = (rows[None, :] == rows[:, None]) & (slots[None, :] < slots[:, None])
    rank = jnp.sum(earlier.astype(jnp.int32), axis=1)
    counts = jnp.sum((rows[None, :] == jnp.arange(4, dtype=jnp.int32)[:, None]).astype(jnp.int32), axis=1)
    ends = jnp.sum(
        jnp.where(
            jnp.arange(4)[None, :] <= jnp.arange(4)[:, None], ((counts + DEEP - 1) // DEEP * DEEP)[None, :], 0
        ),
        axis=1,
    )
    start = jnp.zeros_like(rows)
    for row in range(1, 4):
        start = jnp.where(rows == row, ends[row - 1], start)
    place = jnp.where(rows < 4, start + rank, -1)
    hit = place[None, :] == jnp.arange(DEEP * GROUPS, dtype=jnp.int32)[:, None]
    codes = jnp.sum(jnp.where(hit, (slots * 1024 + blocks - ZERO)[None, :], 0), axis=1) + ZERO
    begin = DEEP * jnp.arange(GROUPS, dtype=jnp.int32)
    product_rows = jnp.sum((begin[:, None] >= ends[None, :]).astype(jnp.int32), axis=1)
    return jnp.concatenate([codes, product_rows, jnp.stack([ends[3], core])]).astype(jnp.int32)


def hold_kernel(tiles_ref, out_ref, sem):
    copy = pltpu.make_async_copy(tiles_ref, out_ref, sem)
    copy.start()
    copy.wait()


def hold_tiles(tiles):
    return pl.pallas_call(
        hold_kernel,
        out_shape=struct(tiles.shape, tiles.dtype),
        in_specs=[ANY],
        out_specs=VMEM,
        scratch_shapes=[pltpu.SemaphoreType.DMA(())],
        compiler_params=TILES_PARAMS,
        cost_estimate=pl.CostEstimate(flops=0, bytes_accessed=16 * 1024 * 1024, transcendentals=0),
    )(tiles)


def add_products(list_ref, tiles_ref, held, sums):
    def products(step, carry):
        results = []
        for u in range(UNROLL):
            base = (step * UNROLL + u) * DEEP
            codes = [list_ref[base + v] for v in range(DEEP)]
            results.append(
                lax.dot_general(
                    jnp.concatenate([held[code & 1023] for code in codes], axis=1),
                    jnp.concatenate([tiles_ref[code >> 10] for code in codes], axis=1),
                    (((1,), (1,)), ((), ())),
                    preferred_element_type=jnp.float32,
                )
            )
        for u in range(UNROLL):
            row = list_ref[DEEP * GROUPS + step * UNROLL + u]
            sums[row] = sums[row] + results[u]
        return carry

    used = list_ref[(DEEP + 1) * GROUPS]
    lax.fori_loop(0, lax.div(used + DEEP * UNROLL - 1, DEEP * UNROLL), products, 0)


def copy_pieces(pieces, held, sems):
    return [
        pltpu.make_async_copy(piece, held.at[pl.ds(number * PIECE, PIECE)], sems.at[number])
        for number, piece in enumerate(pieces)
    ]


def near_kernel(list_ref, tiles_ref, *refs):
    pieces, (sums, held, sems) = refs[:4], refs[4:]
    copies = copy_pieces(pieces, held, sems)
    for copy in copies:
        copy.start()
    held[ZERO] = jnp.zeros((K, 128), jnp.bfloat16)
    sums[...] = jnp.zeros_like(sums)
    for copy in copies:
        copy.wait()
    add_products(list_ref, tiles_ref, held, sums)


def corner_kernel(list_ref, tiles_ref, before_ref, *refs):
    near, pieces = refs[:4], refs[4:8]
    own_ref, other_ref, held, sums, heads, sems, head_sems = refs[8:]
    copies = copy_pieces(pieces, held, sems) + [
        pltpu.make_async_copy(
            piece.at[pl.ds(0, GRAM)], heads.at[pl.ds(number * GRAM, GRAM)], head_sems.at[number]
        )
        for number, piece in enumerate(near)
    ]
    for copy in copies:
        copy.start()
    held[ZERO] = jnp.zeros((K, 128), jnp.bfloat16)
    sums[...] = before_ref[...]
    for copy in copies:
        copy.wait()
    grams = [
        get_gram(heads.at[pl.ds(number * GRAM, GRAM)])
        + get_gram(held.at[pl.ds(number * PIECE, GRAM)])
        for number in range(4)
    ]
    gram = (grams[0] + grams[1]) + (grams[2] + grams[3])
    own_ref[:, 256:] = gram
    other_ref[:, 256:] = gram
    add_products(list_ref, tiles_ref, held, sums)
    core = list_ref[(DEEP + 1) * GROUPS + 1]
    for half in range(2):
        cols = slice(half * 128, (half + 1) * 128)
        own_ref[:, cols] = sums[2 * core + half]
        other_ref[:, cols] = sums[2 * (1 - core) + half]


def tiles_product(slots, tiles, pieces):
    near, corner = pieces[:4], pieces[4:]
    cost = pl.CostEstimate(flops=2 * K * 128 * 128 * SLOTS, bytes_accessed=16 * 1024 * 1024, transcendentals=0)
    blocks = pltpu.VMEM((ZERO + 1, K, 128), jnp.bfloat16)
    sums = pl.pallas_call(
        near_kernel,
        out_shape=struct((5, K, 128), jnp.float32),
        in_specs=[SMEM, VMEM] + [ANY] * 4,
        out_specs=VMEM,
        scratch_shapes=[blocks, pltpu.SemaphoreType.DMA((4,))],
        compiler_params=TILES_PARAMS,
        cost_estimate=cost,
    )(slots[0], tiles, *near)
    return pl.pallas_call(
        corner_kernel,
        out_shape=[struct((K, 384), jnp.float32)] * 2,
        in_specs=[SMEM, VMEM, VMEM] + [ANY] * 8,
        out_specs=[VMEM] * 2,
        scratch_shapes=[
            blocks,
            pltpu.VMEM((5, K, 128), jnp.float32),
            pltpu.VMEM((4 * GRAM, K, 128), jnp.bfloat16),
            pltpu.SemaphoreType.DMA((4,)),
            pltpu.SemaphoreType.DMA((4,)),
        ],
        compiler_params=TILES_PARAMS,
        cost_estimate=cost,
    )(slots[1], tiles, sums, *near, *corner)


def eliminate(gram, held):
    eye = (
        lax.broadcasted_iota(jnp.int32, (K, K), 0) == lax.broadcasted_iota(jnp.int32, (K, K), 1)
    ).astype(jnp.float32)
    whole = jnp.concatenate([gram, eye], axis=1)
    work = [whole[8 * i : 8 * i + 8] for i in range(8)]
    for j in range(0, K, 4):
        first, offset = j // 8, j % 8
        rows = [work[first][offset + u : offset + u + 1] for u in range(4)]
        heads = [
            [jnp.broadcast_to(rows[u][:, j + v : j + v + 1], (1, 128)) for v in range(4)]
            for u in range(4)
        ]
        later = range(first if offset == 0 else first + 1, 8)
        columns = [
            {i: jnp.broadcast_to(work[i][:, j + u : j + u + 1], (8, 128)) for i in later}
            for u in range(4)
        ]
        scaled = []
        for u in range(4):
            over = 1.0 / heads[u][u]
            for v in range(u + 1, 4):
                part = heads[u][v] * over
                rows[v] = rows[v] - part * rows[u]
                for w in range(v, 4):
                    heads[v][w] = heads[v][w] - part * heads[u][w]
                for i in later:
                    columns[v][i] = columns[v][i] - part * columns[u][i]
            scaled.append(rows[u] * over)
        for i in later:
            work[i] = work[i] - (
                (columns[0][i] * scaled[0] + columns[1][i] * scaled[1])
                + (columns[2][i] * scaled[2] + columns[3][i] * scaled[3])
            )
        for u in range(4):
            held[j + u : j + u + 1] = rows[u] * lax.rsqrt(heads[u][u])


def factorize(both, spread_ref, held):
    square, cross = both[:, :K], both[:, K:]
    eliminate(square - dot_t(cross, cross), held)
    result = held[...]
    down = lax.broadcasted_iota(jnp.int32, (K, K), 0)
    right = lax.broadcasted_iota(jnp.int32, (K, K), 1)
    eye = (down == right).astype(jnp.float32)
    upper = jnp.where(right >= down, result[:, :K], 0.0)
    inverse = jnp.where(right <= down, result[:, K:], 0.0)
    carried = dot(inverse, cross)
    record = jnp.concatenate([cross + SHIFT * eye, upper.T], axis=1)
    diagonal = jnp.sum(square * eye, axis=1, keepdims=True)
    spread = dot(inverse * inverse, jnp.broadcast_to(diagonal, (K, 128))) + dot(
        carried * carried, spread_ref[0]
    )
    good = jnp.where(spread < AMPLIFY_MAX, spread_ref[1], 0.0)
    return upper, inverse, carried, record, spread, good


def step_kernel(first, last, own_ref, other_ref, spread_ref, degrees_ref, block_ref, *refs):
    if not first:
        basis_ref, product_ref = refs[:2]
        refs = refs[2:]
    new_block_ref, new_basis_ref, new_product_ref, record_ref, spread_out_ref, packed_ref, held = refs
    both = own_ref[...] + other_ref[...]
    upper, inverse, carried, record, spread, good = factorize(both[:, 256:], spread_ref, held)
    record_ref[...] = record
    spread_out_ref[0] = spread
    spread_out_ref[1] = good
    new_basis = dot(inverse, block_ref[...])
    new_product = dot(inverse, both[:, :256])
    if not first:
        new_basis = new_basis - dot(carried, basis_ref[...])
        new_product = new_product - dot(carried, product_ref[...])
    block = (degrees_ref[...] - SHIFT) * new_basis - new_product
    if not first:
        block = block - dot(upper, basis_ref[...])
    new_block_ref[...] = block
    new_basis_ref[...] = new_basis
    new_product_ref[...] = new_product
    gram = dot_t(block, jnp.concatenate([block, new_basis], axis=0)) * (1.0 / NODES)
    if last:
        packed_ref[...] = gram
    else:
        put_gram(packed_ref, gram)
        put_block(packed_ref, block)


def step(last, own, other, spread, degrees, block, *earlier):
    wide = struct((K, 256), jnp.float32)
    return pl.pallas_call(
        functools.partial(step_kernel, not earlier, last),
        out_shape=[
            wide,
            wide,
            wide,
            struct((K, 128), jnp.float32),
            struct((2, K, 128), jnp.float32),
            struct((K, 128), jnp.float32) if last else struct((GRAM + 2, K, 128), jnp.bfloat16),
        ],
        in_specs=[VMEM] * (5 + len(earlier)),
        out_specs=[VMEM] * 6,
        scratch_shapes=[pltpu.VMEM((K, 128), jnp.float32)],
        compiler_params=SMALL_PARAMS,
    )(own, other, spread, degrees, block, *earlier)


def last_kernel(
    core_ref, own_ref, other_ref, spread_ref, block_ref, basis_ref, first_ref, second_ref,
    out_ref, records_ref, good_ref, held,
):
    own, other = own_ref[...], other_ref[...]
    first_core = core_ref[0] == 0
    gram = jnp.concatenate(
        [jnp.where(first_core, own, other), jnp.where(first_core, other, own)], axis=0
    )
    _, inverse, carried, record, _, good = factorize(gram, spread_ref, held)
    out_ref[...] = dot(inverse, block_ref[...]) - dot(carried, basis_ref[...])
    records_ref[0] = first_ref[...]
    records_ref[1] = second_ref[...]
    records_ref[2] = record
    good_ref[0, 0] = jnp.min(good)


def total_over_chips(value):
    for axis, masks in (("x", (1, 2, 3)), ("y", (1, 2, 3)), ("z", (2, 4, 6)), ("z", (1,))):
        parts = [value] + [swap(value, axis, mask) for mask in masks]
        value = parts[0] + parts[1]
        if len(parts) == 4:
            value = value + (parts[2] + parts[3])
    return value


def short_path(tiles, tile_rows, tile_cols, tile_counts, degrees, start_block):
    y, z, x, core = (lax.axis_index(axis) for axis in AXES)
    live = tile_counts.reshape(())
    tile_set = hold_tiles(tiles.reshape(SLOTS, 128, 128))
    half, blocks = block_index(tile_cols.reshape(-1), y, z, x)
    alive = jnp.arange(SLOTS, dtype=jnp.int32) < live
    slots = [
        slot_list(tile_rows.reshape(-1), blocks, alive & (half == number), core) for number in range(2)
    ]
    degrees = degrees.reshape(1, -1)

    packed = pl.pallas_call(
        first_kernel,
        out_shape=struct((GRAM + 2, K, 128), jnp.bfloat16),
        in_specs=[VMEM],
        out_specs=VMEM,
        compiler_params=SMALL_PARAMS,
    )(start_block)
    block = start_block
    earlier = ()
    spread = jnp.stack([jnp.zeros((K, 128), jnp.float32), jnp.ones((K, 128), jnp.float32)])
    records = []
    for sweep in range(ITERS):
        own, other = tiles_product(slots, tile_set, gather(packed))
        block, basis, product, record, spread, packed = step(
            sweep == ITERS - 1, own, swap(other, "core", 1), spread, degrees, block, *earlier
        )
        earlier = (basis, product)
        records.append(record)
    both = packed + swap(packed, "core", 1)
    share = total_over_chips(lax.dynamic_slice_in_dim(both, core * (K // 2), K // 2, 0))
    basis, records, good = pl.pallas_call(
        last_kernel,
        out_shape=[
            struct((K, 256), jnp.float32),
            struct((ITERS, K, 128), jnp.float32),
            struct((1, 1), jnp.float32),
        ],
        in_specs=[SMEM] + [VMEM] * 7,
        out_specs=[VMEM, VMEM, SMEM],
        compiler_params=SMALL_PARAMS,
        scratch_shapes=[pltpu.VMEM((K, 128), jnp.float32)],
    )(core.astype(jnp.int32).reshape(1), share, swap(share, "core", 1), spread, block, basis, *records[1:])
    return basis, records, good[0, 0]


def tile_terms(totals, blocks, tile_set, row_ids, col_ids, live_count, step_size):
    slab_rows = totals.shape[1]

    def one_block(block_id, running):
        offset = block_id * step_size
        part_tiles = lax.dynamic_slice_in_dim(tile_set, offset, step_size, 0)
        part_rows = lax.dynamic_slice_in_dim(row_ids, offset, step_size, 0)
        part_cols = lax.dynamic_slice_in_dim(col_ids, offset, step_size, 0)
        slot_ids = offset + jnp.arange(step_size, dtype=jnp.int32)
        columns = jnp.take(blocks, part_cols, axis=1)
        contrib = jnp.einsum(
            "ktj,tij->tki", columns, part_tiles, preferred_element_type=jnp.float32
        )
        onehot = (
            (part_rows[:, None] == jnp.arange(slab_rows, dtype=jnp.int32)[None, :])
            & (slot_ids < live_count)[:, None]
        ).astype(jnp.float32)
        return running + jnp.einsum("tr,tki->kri", onehot, contrib, precision=HIGH)

    return lax.fori_loop(0, tile_set.shape[0] // step_size, one_block, totals)


def plain_factorize(block, gram_matrix):
    factor_low = jnp.linalg.cholesky(gram_matrix)
    new_basis = jax.scipy.linalg.solve_triangular(factor_low, block, lower=True)
    return (new_basis, factor_low)


def plain_path(tiles, tile_rows, tile_cols, tile_counts, degrees, start_block):
    vectors = start_block.shape[0]
    own_cols = start_block.shape[1]
    slab_rows = 2 * (own_cols // 128)
    tile_set = tiles.reshape(tiles.shape[2], 128, 128)
    row_ids = tile_rows.reshape(-1)
    col_ids = tile_cols.reshape(-1)
    live_count = tile_counts.reshape(())

    def gram_of(left, right):
        return lax.psum(jnp.dot(left, right.T, precision=HIGH), AXES) / NODES

    basis, factor_low = plain_factorize(start_block, gram_of(start_block, start_block))
    previous = jnp.zeros_like(basis)
    coupling = jnp.zeros((vectors, vectors), jnp.float32)
    records = []
    for sweep in range(ITERS):
        blocks = lax.all_gather(
            basis.astype(jnp.bfloat16), ("y", "z", "x"), axis=1, tiled=True
        ).reshape(vectors, -1, 128)
        totals = jnp.zeros((vectors, slab_rows, 128), jnp.float32)
        totals = tile_terms(totals, blocks, tile_set, row_ids, col_ids, live_count, 32)
        product = lax.psum_scatter(
            totals.reshape(vectors, slab_rows * 128), "core", scatter_dimension=1, tiled=True
        )
        image_block = degrees[None, :] * basis - product
        diag_block = gram_of(image_block, basis)
        residual = (
            image_block
            - jnp.dot(diag_block, basis, precision=HIGH)
            - jnp.dot(coupling, previous, precision=HIGH)
        )
        new_basis, factor_low = plain_factorize(residual, gram_of(residual, residual))
        records.append(jnp.concatenate([diag_block, factor_low], axis=1))
        previous, basis, coupling = (basis, new_basis, factor_low.T)
    return (basis, jnp.stack(records))


def body(*args):
    basis, records, good = short_path(*args)
    return lax.cond(good > 0.5, lambda *rest: (basis, records), plain_path, *args)


def solution(mesh):
    split = Mesh(mesh.devices.reshape(tuple(SIZES[axis] for axis in AXES)), AXES)
    row = ("y", "z", "x")
    in_specs = (
        P(row, "core", None, None, None),
        P(row, "core", None),
        P(row, "core", None),
        P(row, "core"),
        P(AXES),
        P(None, AXES),
    )
    out_specs = (P(None, AXES), P())
    return jax.shard_map(body, mesh=split, in_specs=in_specs, out_specs=out_specs, check_vma=False)
```

```python
import functools

import jax
import jax.numpy as jnp
from jax import lax
from jax.experimental import pallas as pl
from jax.experimental.pallas import tpu as pltpu
from jax.sharding import Mesh, PartitionSpec as P

ITERS = 3
HIGH = lax.Precision.HIGHEST

K = 64
SLOTS = 256
NODES = 65536
SIZES = {"y": 4, "z": 8, "x": 4, "core": 2}
AXES = ("y", "z", "x", "core")
SHIFT = 1.25
AMPLIFY_MAX = 4.0
GRAM = 2

TILES_PARAMS = pltpu.CompilerParams(vmem_limit_bytes=12 * 1024 * 1024)
SMALL_PARAMS = pltpu.CompilerParams(vmem_limit_bytes=4 * 1024 * 1024)

VMEM = pl.BlockSpec(memory_space=pltpu.VMEM)
SMEM = pl.BlockSpec(memory_space=pltpu.SMEM)
ANY = pl.BlockSpec(memory_space=pl.ANY)


def dot(left, right):
    return lax.dot_general(
        left, right, (((1,), (0,)), ((), ())), precision=HIGH, preferred_element_type=jnp.float32
    )


def dot_t(left, right):
    return lax.dot_general(
        left, right, (((1,), (1,)), ((), ())), precision=HIGH, preferred_element_type=jnp.float32
    )


def struct(shape, dtype):
    return jax.ShapeDtypeStruct(shape, dtype)


def put_gram(out_ref, gram):
    high = gram.astype(jnp.bfloat16)
    out_ref[0] = high
    out_ref[1] = (gram - high.astype(jnp.float32)).astype(jnp.bfloat16)


def get_gram(ref):
    return ref[0].astype(jnp.float32) + ref[1].astype(jnp.float32)


def put_block(out_ref, block):
    for half in range(2):
        out_ref[GRAM + half] = block[:, half * 128 : (half + 1) * 128].astype(jnp.bfloat16)


def first_kernel(start_ref, out_ref):
    block = start_ref[...]
    gram = dot_t(block, block) * (1.0 / NODES)
    put_gram(out_ref, jnp.concatenate([gram, jnp.zeros_like(gram)], axis=1))
    put_block(out_ref, block)


def merge_kernel(a_ref, b_ref, c_ref, d_ref, out_ref):
    refs = (a_ref, b_ref, c_ref, d_ref)
    count = a_ref.shape[0] - GRAM
    put_gram(
        out_ref, (get_gram(a_ref) + get_gram(b_ref)) + (get_gram(c_ref) + get_gram(d_ref))
    )
    for place, ref in enumerate(refs):
        out_ref[GRAM + place * count : GRAM + (place + 1) * count] = ref[GRAM:]


def merge(parts):
    count = parts[0].shape[0] - GRAM
    return pl.pallas_call(
        merge_kernel,
        out_shape=struct((GRAM + 4 * count, K, 128), jnp.bfloat16),
        in_specs=[VMEM] * 4,
        out_specs=VMEM,
        compiler_params=SMALL_PARAMS,
    )(*parts)


def swap(value, axis, mask):
    size = SIZES[axis]
    return lax.ppermute(value, axis, [(i, i ^ mask) for i in range(size)])


def send(value, place_of):
    pairs = []
    for y in range(4):
        for z in range(8):
            for x in range(4):
                to_y, to_z, to_x = place_of(y, z, x)
                pairs.append(((y * 8 + z) * 4 + x, (to_y * 8 + to_z) * 4 + to_x))
    return lax.ppermute(value, ("y", "z", "x"), pairs)


def far_z(z):
    return (z + 8 + 2 * (z % 2) - 1) % 8


def gather(packed):
    packed = merge([packed] + [swap(packed, "z", mask) for mask in (2, 4, 6)])
    near = merge(
        [packed]
        + [
            send(packed, lambda y, z, x: (y, z, x ^ 2)),
            send(packed, lambda y, z, x: (y ^ 2, z, x)),
            send(packed, lambda y, z, x: (y ^ 2, z, x ^ 2)),
        ]
    )
    near_x = send(near, lambda y, z, x: (y, z, x ^ 1))
    near_y = send(near, lambda y, z, x: (y ^ 1, z, x))
    near_z = send(near, lambda y, z, x: (y, z ^ 1, x))
    return [
        near,
        near_x,
        near_y,
        near_z,
        send(near, lambda y, z, x: (y ^ 3, far_z(z), x ^ 3)),
        send(near_z, lambda y, z, x: (y ^ 1, z, x)),
        send(near_x, lambda y, z, x: (y, z ^ 1, x)),
        send(near_y, lambda y, z, x: (y, z, x ^ 1)),
    ]


PIECE = GRAM + 32
BUFFER_OF = (0, 1, 2, 7, 3, 6, 5, 4)


def block_index(cols, y, z, x):
    owner = cols // 2
    ys, zs, xs = owner // 32, owner // 4 % 8, owner % 4
    odd_x, odd_y, odd_z = (xs ^ x) & 1, (ys ^ y) & 1, (zs ^ z) & 1
    buffer = jnp.zeros_like(owner)
    for parity, number in enumerate(BUFFER_OF):
        buffer = jnp.where(odd_x + 2 * odd_y + 4 * odd_z == parity, number, buffer)
    corner = buffer == 4
    base_x = x ^ jnp.where(corner, 3 * odd_x, odd_x)
    base_y = y ^ jnp.where(corner, 3 * odd_y, odd_y)
    base_z = jnp.where(odd_z == 0, z, jnp.where(corner, far_z(z), z ^ 1))
    index = ((ys >> 1) ^ (base_y >> 1)) * 8 + ((xs >> 1) ^ (base_x >> 1)) * 4 + ((zs >> 1) ^ (base_z >> 1))
    return buffer // 4, buffer % 4 * PIECE + GRAM + index * 2 + cols % 2


DEEP = 4
UNROLL = 16
GROUPS = (SLOTS + 4 * (DEEP - 1) + DEEP * UNROLL - 1) // (DEEP * UNROLL) * UNROLL
ZERO = 4 * PIECE


def slot_list(rows, blocks, live, core):
    slots = jnp.arange(SLOTS, dtype=jnp.int32)
    rows = jnp.where(live, rows, 4)
    earlier = (rows[None, :] == rows[:, None]) & (slots[None, :] < slots[:, None])
    rank = jnp.sum(earlier.astype(jnp.int32), axis=1)
    counts = jnp.sum((rows[None, :] == jnp.arange(4, dtype=jnp.int32)[:, None]).astype(jnp.int32), axis=1)
    ends = jnp.sum(
        jnp.where(
            jnp.arange(4)[None, :] <= jnp.arange(4)[:, None], ((counts + DEEP - 1) // DEEP * DEEP)[None, :], 0
        ),
        axis=1,
    )
    start = jnp.zeros_like(rows)
    for row in range(1, 4):
        start = jnp.where(rows == row, ends[row - 1], start)
    place = jnp.where(rows < 4, start + rank, -1)
    hit = place[None, :] == jnp.arange(DEEP * GROUPS, dtype=jnp.int32)[:, None]
    codes = jnp.sum(jnp.where(hit, (slots * 1024 + blocks - ZERO)[None, :], 0), axis=1) + ZERO
    begin = DEEP * jnp.arange(GROUPS, dtype=jnp.int32)
    product_rows = jnp.sum((begin[:, None] >= ends[None, :]).astype(jnp.int32), axis=1)
    return jnp.concatenate([codes, product_rows, jnp.stack([ends[3], core])]).astype(jnp.int32)


def hold_kernel(tiles_ref, out_ref, sem):
    copy = pltpu.make_async_copy(tiles_ref, out_ref, sem)
    copy.start()
    copy.wait()


def hold_tiles(tiles):
    return pl.pallas_call(
        hold_kernel,
        out_shape=struct(tiles.shape, tiles.dtype),
        in_specs=[ANY],
        out_specs=VMEM,
        scratch_shapes=[pltpu.SemaphoreType.DMA(())],
        compiler_params=TILES_PARAMS,
        cost_estimate=pl.CostEstimate(flops=0, bytes_accessed=16 * 1024 * 1024, transcendentals=0),
    )(tiles)


def add_products(list_ref, tiles_ref, held, sums):
    def products(step, carry):
        results = []
        for u in range(UNROLL):
            base = (step * UNROLL + u) * DEEP
            codes = [list_ref[base + v] for v in range(DEEP)]
            results.append(
                lax.dot_general(
                    jnp.concatenate([held[code & 1023] for code in codes], axis=1),
                    jnp.concatenate([tiles_ref[code >> 10] for code in codes], axis=1),
                    (((1,), (1,)), ((), ())),
                    preferred_element_type=jnp.float32,
                )
            )
        for u in range(UNROLL):
            row = list_ref[DEEP * GROUPS + step * UNROLL + u]
            sums[row] = sums[row] + results[u]
        return carry

    used = list_ref[(DEEP + 1) * GROUPS]
    lax.fori_loop(0, lax.div(used + DEEP * UNROLL - 1, DEEP * UNROLL), products, 0)


def copy_pieces(pieces, held, sems):
    return [
        pltpu.make_async_copy(piece, held.at[pl.ds(number * PIECE, PIECE)], sems.at[number])
        for number, piece in enumerate(pieces)
    ]


def near_kernel(list_ref, tiles_ref, *refs):
    pieces, (sums, held, sems) = refs[:4], refs[4:]
    copies = copy_pieces(pieces, held, sems)
    for copy in copies:
        copy.start()
    held[ZERO] = jnp.zeros((K, 128), jnp.bfloat16)
    sums[...] = jnp.zeros_like(sums)
    for copy in copies:
        copy.wait()
    add_products(list_ref, tiles_ref, held, sums)


def corner_kernel(list_ref, tiles_ref, before_ref, *refs):
    near, pieces = refs[:4], refs[4:8]
    own_ref, other_ref, held, sums, heads, sems, head_sems = refs[8:]
    copies = copy_pieces(pieces, held, sems) + [
        pltpu.make_async_copy(
            piece.at[pl.ds(0, GRAM)], heads.at[pl.ds(number * GRAM, GRAM)], head_sems.at[number]
        )
        for number, piece in enumerate(near)
    ]
    for copy in copies:
        copy.start()
    held[ZERO] = jnp.zeros((K, 128), jnp.bfloat16)
    sums[...] = before_ref[...]
    for copy in copies:
        copy.wait()
    grams = [
        get_gram(heads.at[pl.ds(number * GRAM, GRAM)])
        + get_gram(held.at[pl.ds(number * PIECE, GRAM)])
        for number in range(4)
    ]
    gram = (grams[0] + grams[1]) + (grams[2] + grams[3])
    own_ref[:, 256:] = gram
    other_ref[:, 256:] = gram
    add_products(list_ref, tiles_ref, held, sums)
    core = list_ref[(DEEP + 1) * GROUPS + 1]
    for half in range(2):
        cols = slice(half * 128, (half + 1) * 128)
        own_ref[:, cols] = sums[2 * core + half]
        other_ref[:, cols] = sums[2 * (1 - core) + half]


def tiles_product(slots, tiles, pieces):
    near, corner = pieces[:4], pieces[4:]
    cost = pl.CostEstimate(flops=2 * K * 128 * 128 * SLOTS, bytes_accessed=16 * 1024 * 1024, transcendentals=0)
    blocks = pltpu.VMEM((ZERO + 1, K, 128), jnp.bfloat16)
    sums = pl.pallas_call(
        near_kernel,
        out_shape=struct((5, K, 128), jnp.float32),
        in_specs=[SMEM, VMEM] + [ANY] * 4,
        out_specs=VMEM,
        scratch_shapes=[blocks, pltpu.SemaphoreType.DMA((4,))],
        compiler_params=TILES_PARAMS,
        cost_estimate=cost,
    )(slots[0], tiles, *near)
    return pl.pallas_call(
        corner_kernel,
        out_shape=[struct((K, 384), jnp.float32)] * 2,
        in_specs=[SMEM, VMEM, VMEM] + [ANY] * 8,
        out_specs=[VMEM] * 2,
        scratch_shapes=[
            blocks,
            pltpu.VMEM((5, K, 128), jnp.float32),
            pltpu.VMEM((4 * GRAM, K, 128), jnp.bfloat16),
            pltpu.SemaphoreType.DMA((4,)),
            pltpu.SemaphoreType.DMA((4,)),
        ],
        compiler_params=TILES_PARAMS,
        cost_estimate=cost,
    )(slots[1], tiles, sums, *near, *corner)


def eliminate(gram, held):
    eye = (
        lax.broadcasted_iota(jnp.int32, (K, K), 0) == lax.broadcasted_iota(jnp.int32, (K, K), 1)
    ).astype(jnp.float32)
    whole = jnp.concatenate([gram, eye], axis=1)
    work = [whole[8 * i : 8 * i + 8] for i in range(8)]
    for j in range(0, K, 4):
        first, offset = j // 8, j % 8
        rows = [work[first][offset + u : offset + u + 1] for u in range(4)]
        heads = [
            [jnp.broadcast_to(rows[u][:, j + v : j + v + 1], (1, 128)) for v in range(4)]
            for u in range(4)
        ]
        later = range(first if offset == 0 else first + 1, 8)
        columns = [
            {i: jnp.broadcast_to(work[i][:, j + u : j + u + 1], (8, 128)) for i in later}
            for u in range(4)
        ]
        scaled = []
        for u in range(4):
            over = 1.0 / heads[u][u]
            for v in range(u + 1, 4):
                part = heads[u][v] * over
                rows[v] = rows[v] - part * rows[u]
                for w in range(v, 4):
                    heads[v][w] = heads[v][w] - part * heads[u][w]
                for i in later:
                    columns[v][i] = columns[v][i] - part * columns[u][i]
            scaled.append(rows[u] * over)
        for i in later:
            work[i] = work[i] - (
                (columns[0][i] * scaled[0] + columns[1][i] * scaled[1])
                + (columns[2][i] * scaled[2] + columns[3][i] * scaled[3])
            )
        for u in range(4):
            held[j + u : j + u + 1] = rows[u] * lax.rsqrt(heads[u][u])


def factorize(both, spread_ref, held):
    square, cross = both[:, :K], both[:, K:]
    eliminate(square - dot_t(cross, cross), held)
    result = held[...]
    down = lax.broadcasted_iota(jnp.int32, (K, K), 0)
    right = lax.broadcasted_iota(jnp.int32, (K, K), 1)
    eye = (down == right).astype(jnp.float32)
    upper = jnp.where(right >= down, result[:, :K], 0.0)
    inverse = jnp.where(right <= down, result[:, K:], 0.0)
    carried = dot(inverse, cross)
    record = jnp.concatenate([cross + SHIFT * eye, upper.T], axis=1)
    diagonal = jnp.sum(square * eye, axis=1, keepdims=True)
    spread = dot(inverse * inverse, jnp.broadcast_to(diagonal, (K, 128))) + dot(
        carried * carried, spread_ref[0]
    )
    good = jnp.where(spread < AMPLIFY_MAX, spread_ref[1], 0.0)
    return upper, inverse, carried, record, spread, good


def step_kernel(first, last, own_ref, other_ref, spread_ref, degrees_ref, block_ref, *refs):
    if not first:
        basis_ref, product_ref = refs[:2]
        refs = refs[2:]
    new_block_ref, new_basis_ref, new_product_ref, record_ref, spread_out_ref, packed_ref, held = refs
    both = own_ref[...] + other_ref[...]
    upper, inverse, carried, record, spread, good = factorize(both[:, 256:], spread_ref, held)
    record_ref[...] = record
    spread_out_ref[0] = spread
    spread_out_ref[1] = good
    new_basis = dot(inverse, block_ref[...])
    new_product = dot(inverse, both[:, :256])
    if not first:
        new_basis = new_basis - dot(carried, basis_ref[...])
        new_product = new_product - dot(carried, product_ref[...])
    block = (degrees_ref[...] - SHIFT) * new_basis - new_product
    if not first:
        block = block - dot(upper, basis_ref[...])
    new_block_ref[...] = block
    new_basis_ref[...] = new_basis
    new_product_ref[...] = new_product
    gram = dot_t(block, jnp.concatenate([block, new_basis], axis=0)) * (1.0 / NODES)
    if last:
        packed_ref[...] = gram
    else:
        put_gram(packed_ref, gram)
        put_block(packed_ref, block)


def step(last, own, other, spread, degrees, block, *earlier):
    wide = struct((K, 256), jnp.float32)
    return pl.pallas_call(
        functools.partial(step_kernel, not earlier, last),
        out_shape=[
            wide,
            wide,
            wide,
            struct((K, 128), jnp.float32),
            struct((2, K, 128), jnp.float32),
            struct((K, 128), jnp.float32) if last else struct((GRAM + 2, K, 128), jnp.bfloat16),
        ],
        in_specs=[VMEM] * (5 + len(earlier)),
        out_specs=[VMEM] * 6,
        scratch_shapes=[pltpu.VMEM((K, 128), jnp.float32)],
        compiler_params=SMALL_PARAMS,
    )(own, other, spread, degrees, block, *earlier)


def last_kernel(
    core_ref, own_ref, other_ref, spread_ref, block_ref, basis_ref, first_ref, second_ref,
    out_ref, records_ref, good_ref, held,
):
    own, other = own_ref[...], other_ref[...]
    first_core = core_ref[0] == 0
    gram = jnp.concatenate(
        [jnp.where(first_core, own, other), jnp.where(first_core, other, own)], axis=0
    )
    _, inverse, carried, record, _, good = factorize(gram, spread_ref, held)
    out_ref[...] = dot(inverse, block_ref[...]) - dot(carried, basis_ref[...])
    records_ref[0] = first_ref[...]
    records_ref[1] = second_ref[...]
    records_ref[2] = record
    good_ref[0, 0] = jnp.min(good)


def total_over_chips(value):
    for axis, masks in (("x", (1, 2, 3)), ("y", (1, 2, 3)), ("z", (2, 4, 6)), ("z", (1,))):
        parts = [value] + [swap(value, axis, mask) for mask in masks]
        value = parts[0] + parts[1]
        if len(parts) == 4:
            value = value + (parts[2] + parts[3])
    return value


def short_path(tiles, tile_rows, tile_cols, tile_counts, degrees, start_block):
    y, z, x, core = (lax.axis_index(axis) for axis in AXES)
    live = tile_counts.reshape(())
    tile_set = hold_tiles(tiles.reshape(SLOTS, 128, 128))
    half, blocks = block_index(tile_cols.reshape(-1), y, z, x)
    alive = jnp.arange(SLOTS, dtype=jnp.int32) < live
    slots = [
        slot_list(tile_rows.reshape(-1), blocks, alive & (half == number), core) for number in range(2)
    ]
    degrees = degrees.reshape(1, -1)

    packed = pl.pallas_call(
        first_kernel,
        out_shape=struct((GRAM + 2, K, 128), jnp.bfloat16),
        in_specs=[VMEM],
        out_specs=VMEM,
        compiler_params=SMALL_PARAMS,
    )(start_block)
    block = start_block
    earlier = ()
    spread = jnp.stack([jnp.zeros((K, 128), jnp.float32), jnp.ones((K, 128), jnp.float32)])
    records = []
    for sweep in range(ITERS):
        own, other = tiles_product(slots, tile_set, gather(packed))
        block, basis, product, record, spread, packed = step(
            sweep == ITERS - 1, own, swap(other, "core", 1), spread, degrees, block, *earlier
        )
        earlier = (basis, product)
        records.append(record)
    both = packed + swap(packed, "core", 1)
    share = total_over_chips(lax.dynamic_slice_in_dim(both, core * (K // 2), K // 2, 0))
    basis, records, good = pl.pallas_call(
        last_kernel,
        out_shape=[
            struct((K, 256), jnp.float32),
            struct((ITERS, K, 128), jnp.float32),
            struct((1, 1), jnp.float32),
        ],
        in_specs=[SMEM] + [VMEM] * 7,
        out_specs=[VMEM, VMEM, SMEM],
        compiler_params=SMALL_PARAMS,
        scratch_shapes=[pltpu.VMEM((K, 128), jnp.float32)],
    )(core.astype(jnp.int32).reshape(1), share, swap(share, "core", 1), spread, block, basis, *records[1:])
    return basis, records, good[0, 0]


def tile_terms(totals, blocks, tile_set, row_ids, col_ids, live_count, step_size):
    slab_rows = totals.shape[1]

    def one_block(block_id, running):
        offset = block_id * step_size
        part_tiles = lax.dynamic_slice_in_dim(tile_set, offset, step_size, 0)
        part_rows = lax.dynamic_slice_in_dim(row_ids, offset, step_size, 0)
        part_cols = lax.dynamic_slice_in_dim(col_ids, offset, step_size, 0)
        slot_ids = offset + jnp.arange(step_size, dtype=jnp.int32)
        columns = jnp.take(blocks, part_cols, axis=1)
        contrib = jnp.einsum(
            "ktj,tij->tki", columns, part_tiles, preferred_element_type=jnp.float32
        )
        onehot = (
            (part_rows[:, None] == jnp.arange(slab_rows, dtype=jnp.int32)[None, :])
            & (slot_ids < live_count)[:, None]
        ).astype(jnp.float32)
        return running + jnp.einsum("tr,tki->kri", onehot, contrib, precision=HIGH)

    return lax.fori_loop(0, tile_set.shape[0] // step_size, one_block, totals)


def plain_factorize(block, gram_matrix):
    factor_low = jnp.linalg.cholesky(gram_matrix)
    new_basis = jax.scipy.linalg.solve_triangular(factor_low, block, lower=True)
    return (new_basis, factor_low)


def plain_path(tiles, tile_rows, tile_cols, tile_counts, degrees, start_block):
    vectors = start_block.shape[0]
    own_cols = start_block.shape[1]
    slab_rows = 2 * (own_cols // 128)
    tile_set = tiles.reshape(tiles.shape[2], 128, 128)
    row_ids = tile_rows.reshape(-1)
    col_ids = tile_cols.reshape(-1)
    live_count = tile_counts.reshape(())

    def gram_of(left, right):
        return lax.psum(jnp.dot(left, right.T, precision=HIGH), AXES) / NODES

    basis, factor_low = plain_factorize(start_block, gram_of(start_block, start_block))
    previous = jnp.zeros_like(basis)
    coupling = jnp.zeros((vectors, vectors), jnp.float32)
    records = []
    for sweep in range(ITERS):
        blocks = lax.all_gather(
            basis.astype(jnp.bfloat16), ("y", "z", "x"), axis=1, tiled=True
        ).reshape(vectors, -1, 128)
        totals = jnp.zeros((vectors, slab_rows, 128), jnp.float32)
        totals = tile_terms(totals, blocks, tile_set, row_ids, col_ids, live_count, 32)
        product = lax.psum_scatter(
            totals.reshape(vectors, slab_rows * 128), "core", scatter_dimension=1, tiled=True
        )
        image_block = degrees[None, :] * basis - product
        diag_block = gram_of(image_block, basis)
        residual = (
            image_block
            - jnp.dot(diag_block, basis, precision=HIGH)
            - jnp.dot(coupling, previous, precision=HIGH)
        )
        new_basis, factor_low = plain_factorize(residual, gram_of(residual, residual))
        records.append(jnp.concatenate([diag_block, factor_low], axis=1))
        previous, basis, coupling = (basis, new_basis, factor_low.T)
    return (basis, jnp.stack(records))


def body(*args):
    basis, records, good = short_path(*args)
    return lax.cond(good > 0.5, lambda *rest: (basis, records), plain_path, *args)


def solution(mesh):
    split = Mesh(mesh.devices.reshape(tuple(SIZES[axis] for axis in AXES)), AXES)
    row = ("y", "z", "x")
    in_specs = (
        P(row, "core", None, None, None),
        P(row, "core", None),
        P(row, "core", None),
        P(row, "core"),
        P(AXES),
        P(None, AXES),
    )
    out_specs = (P(None, AXES), P())
    return jax.shard_map(body, mesh=split, in_specs=in_specs, out_specs=out_specs, check_vma=False)
```
